32 devices in a mesh: req: 8 (over z, y), head: 4 (over x, core).
Axes of the slice: x: 2, y: 2, z: 4, core: 2. Of those that a mesh axis runs over, the one named last changes fastest.
Arguments:
- hidden_in: bfloat16 [128, 2048], P(None, 'req'), may hold values from -6 to 6
- lengths: int32 [128], P('req'), may hold values from 16 to 3072, as said below
- w_qkv: bfloat16 [3, 2048, 2048], P(None, 'req', 'head'), may hold values from -4 to 4, as said below
- qk_gain: float32 [2, 2048], P(None, 'head'), may hold values from 0.25 to 1.75
- cache_keys: bfloat16 [32768, 2048], P('req', 'head'), may hold values from -240 to 240
- cache_values: bfloat16 [32768, 2048], P('req', 'head'), may hold values from -6 to 6
- w_out: bfloat16 [2048, 2048], P('req', 'head'), may hold values from -3 to 3, as said below
- norm_gain: float32 [2, 2048], P(None, 'req'), may hold values from 0.25 to 1.75
- w_gate_up: bfloat16 [2, 2048, 8192], P(None, 'req', 'head'), may hold values from -0.125 to 0.125
- w_down: bfloat16 [2048, 8192], P('req', 'head'), may hold values from -3 to 3, as said below
Outputs:
- hidden_out: bfloat16 [128, 2048], P(None, 'req')
- new_keys: bfloat16 [128, 2048], P('req', 'head')
- new_values: bfloat16 [128, 2048], P('req', 'head')
The draws below stay inside these ranges and needn't reach their ends.
Inputs may be any that keep to these rules, and one draw needn't show every extreme that they name: `lengths`: in each aligned group of requests 8 * 16 * k to 8 * 16 * k + 8 * 16 - 1 exactly one request, at a place drawn from the seed, has length 3072; every other length lies between 16 and 64. `w_qkv`: entries have magnitude at most 26 / sqrt(2048). `w_out`: entries have magnitude at most 23 / sqrt(2048). `w_down`: entries have magnitude at most 23 / sqrt(8192).
All inputs are finite; a program needn't handle non-finite values.
Results may differ from the reference program's by a relative error of at most 0.015.
Values may be sent and summed in bfloat16 or wider, within the bound.
A program may use at most 128 MiB of HBM per device.

```python
import jax
import jax.numpy as jnp
from jax import lax

D = 2048
HEADS = 16
HEAD_DIM = 128
FF = 8192
REQ_DEV = 16
SHORT_MAX = 64
LONG = 3072
REQUESTS = 128
POOL_DEV = 4096
POOL = 32768
N_REQ = 8


def draw_lengths(key, part):
    first, second = jax.random.split(key)
    drawn = jax.random.randint(first, (REQUESTS,), SHORT_MAX // 4, SHORT_MAX + 1)
    span = 8 * REQ_DEV
    groups = REQUESTS // span
    picked = jax.random.randint(second, (groups,), 0, span)
    places = jnp.arange(REQUESTS, dtype=jnp.int32)
    chosen = places % span == picked[places // span]
    return jnp.where(chosen, LONG, drawn).astype(jnp.int32)


def draw_w_qkv(key, part):
    first, second = jax.random.split(jax.random.fold_in(key, 7))
    columns = jnp.arange(D, dtype=jnp.float32)[None, None, :] / D - 0.5
    jitter = jax.random.uniform(second, (3, 1, D), jnp.float32, -0.3, 0.3)
    base = jnp.clip(jax.random.normal(first, (3, D, D), jnp.float32), -6.0, 6.0)
    factor = jnp.exp(jnp.log(4.0) * columns + jitter)
    return (base * factor * D ** (-0.5)).astype(jnp.bfloat16)


def draw_cache_keys(key, part):
    first = jax.random.fold_in(key, 0)
    base = jnp.clip(jax.random.normal(first, (POOL, D), jnp.float32), -6.0, 6.0)
    return base.astype(jnp.bfloat16)


def scaled_rows(key, rows_total, cols_total):
    first, second = jax.random.split(key)
    base = jnp.clip(jax.random.normal(first, (rows_total, cols_total), jnp.float32), -6.0, 6.0)
    spread = jax.random.uniform(second, (rows_total, 1), jnp.float32, -1.15, 1.15)
    rising = jnp.log(3.0) * (jnp.arange(rows_total, dtype=jnp.float32)[:, None] / rows_total - 0.5)
    return base * jnp.exp(spread + rising) * cols_total ** (-0.5) / 1.47


def draw_w_out(key, part):
    return scaled_rows(key, D, D).astype(jnp.bfloat16)


def draw_w_down(key, part):
    return scaled_rows(key, D, FF).astype(jnp.bfloat16)


def steps_of(key, shape, pieces, low, high):
    def one(dim, shards_of):
        draws = jax.random.uniform(jax.random.fold_in(jax.random.fold_in(key, 6), dim), (shards_of,), jnp.float32, low / len(pieces), high / len(pieces))
        return jnp.repeat(jnp.exp(draws), shape[dim] // shards_of).reshape((-1,) + (1,) * (len(shape) - dim - 1))

    level = one(*pieces[0])
    for cut in pieces[1:]:
        level = level * one(*cut)
    return level


def scatter_about(rng, shape, deviation, limit, pieces=(), kind=jnp.bfloat16):
    values = deviation * jax.random.normal(rng, shape, jnp.float32)
    if pieces:
        values = values * steps_of(rng, shape, pieces, -0.22, 0.18)
    return jnp.clip(values, -limit, limit).astype(kind)


def setup_inputs(seed: int = 0) -> dict:
    arg_keys = jax.random.split(jax.random.key(seed), 11)
    hidden_in = scatter_about(arg_keys[0], (REQUESTS, D), 1.0, 6.0, ((1, 8),))
    lengths = draw_lengths(jax.random.fold_in(arg_keys[10], 71), 0)
    w_qkv = draw_w_qkv(jax.random.fold_in(arg_keys[10], 71), 0)
    qk_gain = jnp.clip(1.0 + 0.15 * jax.random.normal(arg_keys[3], (2, D), jnp.float32), 0.25, 1.75)
    cache_keys = draw_cache_keys(jax.random.fold_in(arg_keys[10], 71), 0)
    cache_values = scatter_about(arg_keys[5], (POOL, D), 1.0, 6.0, ((0, 8), (1, 4)))
    w_out = draw_w_out(jax.random.fold_in(arg_keys[10], 71), 0)
    norm_gain = jnp.clip(1.0 + 0.15 * jax.random.normal(arg_keys[7], (2, D), jnp.float32), 0.25, 1.75)
    w_gate_up = scatter_about(arg_keys[8], (2, D, FF), D ** -0.5, 0.125, ((1, 8), (2, 4)))
    w_down = draw_w_down(jax.random.fold_in(arg_keys[10], 71), 0)
    return {"hidden_in": hidden_in, "lengths": lengths, "w_qkv": w_qkv, "qk_gain": qk_gain, "cache_keys": cache_keys, "cache_values": cache_values, "w_out": w_out, "norm_gain": norm_gain, "w_gate_up": w_gate_up, "w_down": w_down}


EPS = 1e-06
THETA = 500000.0

def rotate(values, positions):
    half = values.shape[-1] // 2
    freqs = jnp.power(THETA, -(jnp.arange(half, dtype=jnp.float32) * 2.0 / values.shape[-1]))
    angles = positions.astype(jnp.float32)[:, None] * freqs[None, :]
    cosine = jnp.cos(angles)[:, None, :]
    sine = jnp.sin(angles)[:, None, :]
    first = values[..., :half]
    second = values[..., half:]
    return jnp.concatenate([first * cosine - second * sine, second * cosine + first * sine], axis=-1)

def normalize(values, gain):
    power = lax.optimization_barrier(jnp.mean(values * values, axis=-1, keepdims=True))
    return values * lax.rsqrt(power + EPS) * gain

def attend_device(items):
    query, key_self, value_self, counts, stored_keys, stored_values = items
    scale = HEAD_DIM ** (-0.5)
    starts = jnp.cumsum(counts) - counts
    ends = starts + counts
    positions = jnp.arange(POOL_DEV, dtype=jnp.int32)
    inside = (positions[None, :] >= starts[:, None]) & (positions[None, :] < ends[:, None])
    query_wide = query.astype(jnp.float32)
    scores = jnp.einsum('rhd,phd->rhp', query_wide, stored_keys.astype(jnp.float32)) * scale
    scores = jnp.where(inside[:, None, :], scores, -jnp.inf)
    own_score = lax.optimization_barrier(jnp.sum(query_wide * key_self.astype(jnp.float32), axis=2)) * scale
    highest = jnp.maximum(lax.optimization_barrier(jnp.max(scores, axis=2)), own_score)
    weights = lax.optimization_barrier(jnp.exp(scores - highest[:, :, None]).astype(jnp.bfloat16)).astype(jnp.float32)
    own_weight = lax.optimization_barrier(jnp.exp(own_score - highest).astype(jnp.bfloat16)).astype(jnp.float32)
    denominator = lax.optimization_barrier(jnp.sum(weights, axis=2)) + own_weight
    numerator = jnp.einsum('rhp,phd->rhd', weights, stored_values.astype(jnp.float32))
    numerator = numerator + own_weight[:, :, None] * value_self.astype(jnp.float32)
    return (numerator / denominator[:, :, None]).astype(jnp.bfloat16)

def reference(hidden_in, lengths, w_qkv, qk_gain, cache_keys, cache_values, w_out, norm_gain, w_gate_up, w_down):
    query = jnp.dot(hidden_in, w_qkv[0], preferred_element_type=jnp.float32)
    key_new = jnp.dot(hidden_in, w_qkv[1], preferred_element_type=jnp.float32)
    value_new = jnp.dot(hidden_in, w_qkv[2], preferred_element_type=jnp.float32).astype(jnp.bfloat16)
    query = normalize(query, qk_gain[0])
    key_new = normalize(key_new, qk_gain[1])
    query_rot = rotate(query.reshape(REQUESTS, HEADS, HEAD_DIM), lengths).astype(jnp.bfloat16)
    key_rot = rotate(key_new.reshape(REQUESTS, HEADS, HEAD_DIM), lengths).astype(jnp.bfloat16)
    grouped = (query_rot.reshape(N_REQ, REQ_DEV, HEADS, HEAD_DIM), key_rot.reshape(N_REQ, REQ_DEV, HEADS, HEAD_DIM), value_new.reshape(N_REQ, REQ_DEV, HEADS, HEAD_DIM), lengths.reshape(N_REQ, REQ_DEV), cache_keys.reshape(N_REQ, POOL_DEV, HEADS, HEAD_DIM), cache_values.reshape(N_REQ, POOL_DEV, HEADS, HEAD_DIM))
    attended = lax.map(attend_device, grouped).reshape(REQUESTS, D)
    attn_full = jnp.dot(attended, w_out.T, preferred_element_type=jnp.float32)
    hidden_mid = (hidden_in.astype(jnp.float32) + normalize(attn_full, norm_gain[0])).astype(jnp.bfloat16)
    gated = jnp.dot(hidden_mid, w_gate_up[0], preferred_element_type=jnp.float32)
    lifted = jnp.dot(hidden_mid, w_gate_up[1], preferred_element_type=jnp.float32)
    activated = (jax.nn.silu(gated) * lifted).astype(jnp.bfloat16)
    ffn_full = jnp.dot(activated, w_down.T, preferred_element_type=jnp.float32)
    hidden_out = (hidden_mid.astype(jnp.float32) + normalize(ffn_full, norm_gain[1])).astype(jnp.bfloat16)
    return (hidden_out, key_rot.reshape(REQUESTS, D), value_new)
```

```python
import functools

import jax
import jax.numpy as jnp
import numpy as np
from jax import lax
from jax.experimental import pallas as pl
from jax.experimental.pallas import tpu as pltpu
from jax.sharding import PartitionSpec as P

HEAD_DIM = 128
EPS = 1e-06
THETA = 500000.0
MESH = pl.DeviceIdType.MESH
F32 = jnp.float32
BF16 = jnp.bfloat16
CHUNKS = 4
KEY_BLOCK = 512


def dot(left, right):
    return lax.dot_general(left, right, (((1,), (0,)), ((), ())), preferred_element_type=F32)


def dot_last(left, right):
    return lax.dot_general(left, right, (((1,), (1,)), ((), ())), preferred_element_type=F32)


def kernel(
    n, heads_axis, model_width,
    lens, hid, qkg, ng, freq, wqkv_h, ck_h, cv_h, wout_h, wgu_h, wdn_h,
    out, nk, nv,
    wqkv, ck, cv, wout, wgu, wdn, load_sem,
    hp, pq, yq, sq, zq, pkv, ykv, skv, zkv, rs_send, rs_recv,
    sqs, sqr, sq_send, sq_recv,
    scores, att, att_send, att_recv,
    ar_src, ar_dst, ar_send, ar_recv,
    pw_src, pw_dst, pw_send, pw_recv,
    hm, gp, gy, gs, gz, gy_send, gy_recv, gz_send, gz_recv,
    act, az_send, az_recv, ay_send, ay_recv,
):
    me = lax.axis_index("req")
    hi = lax.axis_index("head")
    m = n // 2
    zi = lax.div(me, 2)
    yi = lax.rem(me, 2)
    rows = lens.shape[0]
    width = qkg.shape[1]
    heads = width // HEAD_DIM
    total_rows = n * rows
    slot = yi * m + zi
    ypart = zi * 2 + (1 - yi)

    def loader(index, src, dst):
        return pltpu.make_async_copy(src, dst, load_sem.at[index])

    loads = [
        loader(0, wqkv_h, wqkv), loader(1, ck_h, ck), loader(2, cv_h, cv),
        loader(3, wout_h, wout), loader(4, wgu_h, wgu), loader(5, wdn_h, wdn),
    ]
    for load in loads:
        load.start()

    barrier = pltpu.get_barrier_semaphore()
    for d in range(1, n):
        pl.semaphore_signal(barrier, inc=1, device_id=(lax.rem(me + d, n), hi), device_id_type=MESH)
    for d in range(1, heads_axis):
        pl.semaphore_signal(
            barrier, inc=1, device_id=(me, lax.rem(hi + d, heads_axis)), device_id_type=MESH
        )

    def send(src, dst, ssem, rsem, req, head):
        copy = pltpu.make_async_remote_copy(
            src_ref=src, dst_ref=dst, send_sem=ssem, recv_sem=rsem,
            device_id=(req, head), device_id_type=MESH,
        )
        copy.start()
        return copy

    pending = []

    for y in range(2):
        for z in range(m):
            hp[pl.ds((y * m + z) * rows, rows), :] = hid[pl.ds((z * 2 + y) * rows, rows), :]
    loads[0].wait()
    x = hp[...]
    pq[...] = dot(x, wqkv[0]).reshape(2, m, rows, width)
    pkv[:, :, :, :width] = dot(x, wqkv[1]).astype(BF16).reshape(2, m, rows, width)
    pkv[:, :, :, width:] = dot(x, wqkv[2]).astype(BF16).reshape(2, m, rows, width)
    pl.semaphore_wait(barrier, n - 1 + heads_axis - 1)
    yq_copy = send(pq.at[1 - yi], yq, rs_send.at[0, 0], rs_recv.at[0, 0], ypart, hi)
    ykv_copy = send(pkv.at[1 - yi], ykv, rs_send.at[1, 0], rs_recv.at[1, 0], ypart, hi)
    pending += [yq_copy, ykv_copy]

    row_id = lax.broadcasted_iota(jnp.int32, (rows, HEAD_DIM), 0)
    lane = lax.broadcasted_iota(jnp.int32, (rows, HEAD_DIM), 1)
    starts = jnp.zeros((rows, HEAD_DIM), jnp.int32)
    lengths = jnp.zeros((rows, HEAD_DIM), jnp.int32)
    at = jnp.int32(0)
    for r in range(rows):
        length = lens[r]
        starts = jnp.where(row_id == r, at, starts)
        lengths = jnp.where(row_id == r, length, lengths)
        at = at + length
    ends = starts + lengths
    angles = lengths.astype(F32) * freq[0:1, :]
    cosine = jnp.cos(angles)
    sine = jnp.sin(angles)
    sine = jnp.where(lane < HEAD_DIM // 2, -sine, sine)

    yq_copy.wait_recv()
    sq[...] = pq[yi] + yq[...]
    zq_copies = []
    for d in range(1, m):
        t = lax.rem(zi + d, m)
        zq_copies.append(
            send(sq.at[t], zq.at[d - 1], rs_send.at[0, d], rs_recv.at[0, d], t * 2 + yi, hi)
        )
    ykv_copy.wait_recv()
    skv[...] = (pkv[yi].astype(F32) + ykv[...].astype(F32)).astype(BF16)
    zkv_copies = []
    for d in range(1, m):
        t = lax.rem(zi + d, m)
        zkv_copies.append(
            send(skv.at[t], zkv.at[d - 1], rs_send.at[1, d], rs_recv.at[1, d], t * 2 + yi, hi)
        )
    pending += zq_copies + zkv_copies
    query = sq[zi]
    for d in range(1, m):
        zq_copies[d - 1].wait_recv()
        query = query + zq[d - 1]
    both = skv[zi].astype(F32)
    for d in range(1, m):
        zkv_copies[d - 1].wait_recv()
        both = both + zkv[d - 1].astype(F32)
    key_new = both[:, :width]
    value_new = both[:, width:].astype(BF16)
    nv[...] = value_new

    q_power = jnp.sum(query * query, axis=1, keepdims=True)
    k_power = jnp.sum(key_new * key_new, axis=1, keepdims=True)
    sqs[...] = jnp.where(lane < HEAD_DIM // 2, q_power, k_power)
    sq_copies = []
    for d in range(1, heads_axis):
        sq_copies.append(
            send(sqs, sqr.at[d - 1], sq_send.at[d - 1], sq_recv.at[d - 1],
                 me, lax.rem(hi + d, heads_axis))
        )
    pending += sq_copies
    powers = sqs[...]
    for d in range(1, heads_axis):
        sq_copies[d - 1].wait_recv()
        powers = powers + sqr[d - 1]
    full_width = width * heads_axis
    scales = lax.rsqrt(powers / full_width + EPS)
    query = query * scales[:, 0:1] * qkg[0:1, :]
    key_new = key_new * scales[:, HEAD_DIM - 1 : HEAD_DIM] * qkg[1:2, :]

    def rotate(values):
        parts = []
        for h in range(heads):
            part = values[:, h * HEAD_DIM : (h + 1) * HEAD_DIM]
            parts.append(part * cosine + pltpu.roll(part, HEAD_DIM // 2, 1) * sine)
        return jnp.concatenate(parts, axis=1)

    query_rot = rotate(query).astype(BF16).astype(F32)
    key_rot = rotate(key_new).astype(BF16)
    nk[...] = key_rot
    key_rot = key_rot.astype(F32)

    scale = HEAD_DIM ** (-0.5)
    wide_lane = lax.broadcasted_iota(jnp.int32, (rows, width), 1)
    q_rows = []
    own = []
    for h in range(heads):
        inside = (wide_lane >= h * HEAD_DIM) & (wide_lane < (h + 1) * HEAD_DIM)
        picked = jnp.where(inside, query_rot, 0.0)
        q_rows.append(picked)
        own.append(jnp.sum(picked * key_rot, axis=1, keepdims=True) * scale)
    q_rows = jnp.concatenate(q_rows, axis=0).astype(BF16)
    own = jnp.concatenate(own, axis=0)
    first = jnp.concatenate([starts[:, 0:1]] * heads, axis=0)
    last = jnp.concatenate([ends[:, 0:1]] * heads, axis=0)
    pool = ck.shape[0]
    loads[1].wait()
    highest = own
    for b in range(pool // KEY_BLOCK):
        span = pl.ds(b * KEY_BLOCK, KEY_BLOCK)
        s = dot_last(q_rows, ck[span, :]) * scale
        place = b * KEY_BLOCK + lax.broadcasted_iota(jnp.int32, s.shape, 1)
        s = jnp.where((place >= first) & (place < last), s, -1e30)
        scores[:, span] = s
        highest = jnp.maximum(highest, jnp.max(s, axis=1, keepdims=True))
    own_weight = jnp.exp(own - highest).astype(BF16).astype(F32)
    denominator = own_weight
    numerator = own_weight * jnp.concatenate([value_new.astype(F32)] * heads, axis=0)
    loads[2].wait()
    for b in range(pool // KEY_BLOCK):
        span = pl.ds(b * KEY_BLOCK, KEY_BLOCK)
        w = jnp.exp(scores[:, span] - highest).astype(BF16)
        denominator = denominator + jnp.sum(w.astype(F32), axis=1, keepdims=True)
        numerator = numerator + dot(w, cv[span, :])
    ratio = numerator / denominator
    attended = jnp.concatenate(
        [
            ratio[h * rows : (h + 1) * rows, h * HEAD_DIM : (h + 1) * HEAD_DIM]
            for h in range(heads)
        ],
        axis=1,
    ).astype(BF16)
    att[slot] = attended
    att_copies = []
    for d in range(1, n):
        t = lax.rem(me + d, n)
        att_copies.append(
            send(att.at[slot], att.at[slot], att_send.at[d - 1], att_recv.at[d - 1], t, hi)
        )
    pending += att_copies
    loads[3].wait()
    for d in range(1, n):
        s = lax.rem(me - d + n, n)
        there = att.at[lax.rem(s, 2) * m + lax.div(s, 2)]
        pltpu.make_async_remote_copy(
            src_ref=there, dst_ref=there, send_sem=att_send.at[d - 1],
            recv_sem=att_recv.at[d - 1], device_id=(s, hi), device_id_type=MESH,
        ).wait_recv()

    def sum_heads(part, which):
        bit = 1
        step = 0
        while bit < heads_axis:
            rounded = part.astype(BF16)
            ar_src[which, step] = rounded
            partner = hi + bit - 2 * bit * lax.rem(lax.div(hi, bit), 2)
            copy = send(ar_src.at[which, step], ar_dst.at[which, step],
                        ar_send.at[which, step], ar_recv.at[which, step], me, partner)
            pending.append(copy)
            copy.wait_recv()
            part = rounded.astype(F32) + ar_dst[which, step].astype(F32)
            bit *= 2
            step += 1
        return part

    eye = lax.broadcasted_iota(jnp.int32, (total_rows, total_rows), 0) == lax.broadcasted_iota(
        jnp.int32, (total_rows, total_rows), 1
    )

    def inverse_rms(part, which):
        power = jnp.sum(part * part, axis=1, keepdims=True)
        flat = jnp.sum(jnp.where(eye, power, 0.0), axis=0, keepdims=True)
        pw_src[which] = jnp.broadcast_to(flat, (8, total_rows))
        copies = []
        for d in range(1, n):
            copies.append(
                send(pw_src.at[which], pw_dst.at[which, d - 1], pw_send.at[which, d - 1],
                     pw_recv.at[which, d - 1], lax.rem(me + d, n), hi)
            )
        pending.extend(copies)
        for d in range(1, n):
            copies[d - 1].wait_recv()
            flat = flat + pw_dst[which, d - 1, 0:1, :]
        scaled = lax.rsqrt(flat / model_width + EPS)
        return jnp.sum(jnp.where(eye, scaled, 0.0), axis=1, keepdims=True)

    attn = sum_heads(dot_last(att[...].reshape(total_rows, width), wout[...]), 0)
    attn = attn * inverse_rms(attn, 0) * ng[0:1, :]
    hm[...] = (hp[...].astype(F32) + attn).astype(BF16)

    units = wgu.shape[2]
    cu = units // CHUNKS
    loads[4].wait()
    gy_copies = []
    for c in range(CHUNKS):
        cols = pl.ds(c * cu, cu)
        gp[c, :, :, :, :cu] = dot(hm[...], wgu[0, :, cols]).astype(BF16).reshape(2, m, rows, cu)
        gp[c, :, :, :, cu:] = dot(hm[...], wgu[1, :, cols]).astype(BF16).reshape(2, m, rows, cu)
        gy_copies.append(
            send(gp.at[c, 1 - yi], gy.at[c], gy_send.at[c], gy_recv.at[c], ypart, hi)
        )
    pending += gy_copies
    gz_copies = {}
    ay_copies = {}
    az_copies = {}
    state = {"down": None}

    def pair_sum(c):
        gy_copies[c].wait_recv()
        gs[c] = (gp[c, yi].astype(F32) + gy[c].astype(F32)).astype(BF16)
        for d in range(1, m):
            t = lax.rem(zi + d, m)
            gz_copies[c, d] = send(gs.at[c, t], gz.at[c, d - 1], gz_send.at[c, d - 1],
                                   gz_recv.at[c, d - 1], t * 2 + yi, hi)
            pending.append(gz_copies[c, d])

    def activate(c):
        full = gs[c, zi].astype(F32)
        for d in range(1, m):
            gz_copies[c, d].wait_recv()
            full = full + gz[c, d - 1].astype(F32)
        gate = full[:, :cu]
        act[c, slot] = (gate / (1.0 + jnp.exp(-gate)) * full[:, cu:]).astype(BF16)
        for d in range(1, m):
            t = lax.rem(zi + d, m)
            az_copies[c, d] = send(act.at[c, slot], act.at[c, slot], az_send.at[c, d - 1],
                                   az_recv.at[c, d - 1], t * 2 + yi, hi)
            pending.append(az_copies[c, d])

    def forward(c):
        for d in range(1, m):
            s = lax.rem(zi - d + m, m)
            there = act.at[c, yi * m + s]
            pltpu.make_async_remote_copy(
                src_ref=there, dst_ref=there, send_sem=az_send.at[c, d - 1],
                recv_sem=az_recv.at[c, d - 1], device_id=(s * 2 + yi, hi), device_id_type=MESH,
            ).wait_recv()
        mine = act.at[c, pl.ds(yi * m, m)]
        ay_copies[c] = send(mine, mine, ay_send.at[c], ay_recv.at[c], ypart, hi)
        pending.append(ay_copies[c])

    def project(c):
        other = act.at[c, pl.ds((1 - yi) * m, m)]
        pltpu.make_async_remote_copy(
            src_ref=other, dst_ref=other, send_sem=ay_send.at[c], recv_sem=ay_recv.at[c],
            device_id=(ypart, hi), device_id_type=MESH,
        ).wait_recv()
        if c == 0:
            loads[5].wait()
        part = dot_last(act[c].reshape(total_rows, cu), wdn[:, pl.ds(c * cu, cu)])
        state["down"] = part if state["down"] is None else state["down"] + part

    stages = (pair_sum, activate, forward, project)
    for step in range(CHUNKS + len(stages) - 1):
        for k, stage in enumerate(stages):
            if 0 <= step - k < CHUNKS:
                stage(step - k)
    ffn = sum_heads(state["down"], 1)
    ffn = ffn * inverse_rms(ffn, 1) * ng[1:2, :]
    result = (hm[...].astype(F32) + ffn).astype(BF16)
    for y in range(2):
        for z in range(m):
            p = (y * m + z) * rows
            out[pl.ds((z * 2 + y) * rows, rows), :] = result[p : p + rows]
    for copy in pending:
        copy.wait_send()


def body(
    n, heads_axis,
    hidden_in, lengths, w_qkv, qk_gain, cache_keys, cache_values,
    w_out, norm_gain, w_gate_up, w_down,
):
    rows = lengths.shape[0]
    total_rows, feat = hidden_in.shape
    width = w_qkv.shape[2]
    heads = width // HEAD_DIM
    units = w_gate_up.shape[2]
    m = n // 2
    cu = units // CHUNKS
    half = HEAD_DIM // 2
    steps = max(1, heads_axis.bit_length() - 1)
    freqs = np.power(THETA, -(np.arange(half, dtype=np.float64) * 2.0 / HEAD_DIM))
    freqs = np.broadcast_to(np.concatenate([freqs, freqs]), (8, HEAD_DIM)).astype(np.float32)
    dma = pltpu.SemaphoreType.DMA
    vmem = pltpu.VMEM
    scratch = [
        vmem(w_qkv.shape, BF16), vmem(cache_keys.shape, BF16), vmem(cache_values.shape, BF16),
        vmem(w_out.shape, BF16), vmem(w_gate_up.shape, BF16), vmem(w_down.shape, BF16), dma((6,)),
        vmem((total_rows, feat), BF16),
        vmem((2, m, rows, width), F32), vmem((m, rows, width), F32),
        vmem((m, rows, width), F32), vmem((m - 1, rows, width), F32),
        vmem((2, m, rows, 2 * width), BF16), vmem((m, rows, 2 * width), BF16),
        vmem((m, rows, 2 * width), BF16), vmem((m - 1, rows, 2 * width), BF16),
        dma((2, m)), dma((2, m)),
        vmem((rows, HEAD_DIM), F32), vmem((heads_axis - 1, rows, HEAD_DIM), F32),
        dma((heads_axis - 1,)), dma((heads_axis - 1,)),
        vmem((heads * rows, cache_keys.shape[0]), F32),
        vmem((n, rows, width), BF16), dma((n - 1,)), dma((n - 1,)),
        vmem((2, steps, total_rows, feat), BF16), vmem((2, steps, total_rows, feat), BF16),
        dma((2, steps)), dma((2, steps)),
        vmem((2, 8, total_rows), F32), vmem((2, n - 1, 8, total_rows), F32),
        dma((2, n - 1)), dma((2, n - 1)),
        vmem((total_rows, feat), BF16),
        vmem((CHUNKS, 2, m, rows, 2 * cu), BF16), vmem((CHUNKS, m, rows, 2 * cu), BF16),
        vmem((CHUNKS, m, rows, 2 * cu), BF16), vmem((CHUNKS, m - 1, rows, 2 * cu), BF16),
        dma((CHUNKS,)), dma((CHUNKS,)), dma((CHUNKS, m - 1)), dma((CHUNKS, m - 1)),
        vmem((CHUNKS, n, rows, cu), BF16),
        dma((CHUNKS, m - 1)), dma((CHUNKS, m - 1)), dma((CHUNKS,)), dma((CHUNKS,)),
    ]
    in_vmem = pl.BlockSpec(memory_space=pltpu.VMEM)
    anywhere = pl.BlockSpec(memory_space=pl.ANY)
    return pl.pallas_call(
        functools.partial(kernel, n, heads_axis, feat * n),
        out_shape=(
            jax.ShapeDtypeStruct((total_rows, feat), BF16),
            jax.ShapeDtypeStruct((rows, width), BF16),
            jax.ShapeDtypeStruct((rows, width), BF16),
        ),
        in_specs=[pl.BlockSpec(memory_space=pltpu.SMEM)] + [in_vmem] * 4 + [anywhere] * 6,
        out_specs=(in_vmem,) * 3,
        scratch_shapes=scratch,
        compiler_params=pltpu.CompilerParams(
            collective_id=0, has_side_effects=True, vmem_limit_bytes=56 * 1024 * 1024
        ),
    )(
        lengths, hidden_in, qk_gain, norm_gain, jnp.asarray(freqs),
        w_qkv, cache_keys, cache_values, w_out, w_gate_up, w_down,
    )


def solution(mesh):
    return jax.shard_map(
        functools.partial(body, mesh.shape["req"], mesh.shape["head"]),
        mesh=mesh,
        in_specs=(
            P(None, "req"),
            P("req"),
            P(None, "req", "head"),
            P(None, "head"),
            P("req", "head"),
            P("req", "head"),
            P("req", "head"),
            P(None, "req"),
            P(None, "req", "head"),
            P("req", "head"),
        ),
        out_specs=(P(None, "req"), P("req", "head"), P("req", "head")),
        check_vma=False,
    )
```

```python
import functools

import jax
import jax.numpy as jnp
import numpy as np
from jax import lax
from jax.experimental import pallas as pl
from jax.experimental.pallas import tpu as pltpu
from jax.sharding import PartitionSpec as P

HEAD_DIM = 128
EPS = 1e-06
THETA = 500000.0
MESH = pl.DeviceIdType.MESH
F32 = jnp.float32
BF16 = jnp.bfloat16
CHUNKS = 4
KEY_BLOCK = 512


def dot(left, right):
    return lax.dot_general(left, right, (((1,), (0,)), ((), ())), preferred_element_type=F32)


def place_outputs(a, b, c, out_a, out_b, out_c, sem):
    pairs = ((a, out_a), (b, out_b), (c, out_c))
    copies = [pltpu.make_async_copy(src, dst, sem.at[i]) for i, (src, dst) in enumerate(pairs)]
    for copy in copies:
        copy.start()
    for copy in copies:
        copy.wait()


def kernel(
    n, heads_axis, model_width,
    lens, hid, qkg, ng, freq, wqkv_h, ck_h, cv_h, wout_h, wgu_h, wdn_h,
    out, nk, nv,
    wqkv, ck, cv, wout, wgu, wdn, wout_t, wdn_t, load_sem,
    hp, pq, yq, sq, zq, pkv, ykv, skv, zkv, rs_send, rs_recv,
    sqs, sqr, sq_send, sq_recv,
    scores, att, att_send, att_recv,
    ar_src, ar_dst, ar_send, ar_recv,
    pw_src, pw_dst, pw_send, pw_recv,
    hm, gp, gy, gs, gz, gy_send, gy_recv, gz_send, gz_recv,
    act, az_send, az_recv, ay_send, ay_recv,
):
    me = lax.axis_index("req")
    hi = lax.axis_index("head")
    m = n // 2
    zi = lax.div(me, 2)
    yi = lax.rem(me, 2)
    rows = lens.shape[0]
    width = qkg.shape[1]
    heads = width // HEAD_DIM
    total_rows = n * rows
    slot = yi * m + zi
    ypart = zi * 2 + (1 - yi)

    def loader(index, src, dst):
        return pltpu.make_async_copy(src, dst, load_sem.at[index])

    loads = [
        loader(0, wqkv_h, wqkv), loader(1, ck_h, ck), loader(2, cv_h, cv),
        loader(3, wout_h, wout), loader(4, wgu_h, wgu), loader(5, wdn_h, wdn),
    ]
    loads[0].start()

    barrier = pltpu.get_barrier_semaphore()
    for d in range(1, n):
        pl.semaphore_signal(barrier, inc=1, device_id=(lax.rem(me + d, n), hi), device_id_type=MESH)
    for d in range(1, heads_axis):
        pl.semaphore_signal(
            barrier, inc=1, device_id=(me, lax.rem(hi + d, heads_axis)), device_id_type=MESH
        )

    def send(src, dst, ssem, rsem, req, head):
        copy = pltpu.make_async_remote_copy(
            src_ref=src, dst_ref=dst, send_sem=ssem, recv_sem=rsem,
            device_id=(req, head), device_id_type=MESH,
        )
        copy.start()
        return copy

    pending = []

    for y in range(2):
        for z in range(m):
            hp[pl.ds((y * m + z) * rows, rows), :] = hid[pl.ds((z * 2 + y) * rows, rows), :]
    loads[0].wait()
    for load in loads[1:]:
        load.start()
    x = hp[...]
    pq[...] = dot(x, wqkv[0]).reshape(2, m, rows, width)
    pl.semaphore_wait(barrier, n - 1 + heads_axis - 1)
    yq_copy = send(pq.at[1 - yi], yq, rs_send.at[0, 0], rs_recv.at[0, 0], ypart, hi)
    pkv[:, :, :, :width] = dot(x, wqkv[1]).astype(BF16).reshape(2, m, rows, width)
    pkv[:, :, :, width:] = dot(x, wqkv[2]).astype(BF16).reshape(2, m, rows, width)
    ykv_copy = send(pkv.at[1 - yi], ykv, rs_send.at[1, 0], rs_recv.at[1, 0], ypart, hi)
    pending += [yq_copy, ykv_copy]

    row_id = lax.broadcasted_iota(jnp.int32, (rows, HEAD_DIM), 0)
    lane = lax.broadcasted_iota(jnp.int32, (rows, HEAD_DIM), 1)
    starts = jnp.zeros((rows, HEAD_DIM), jnp.int32)
    lengths = jnp.zeros((rows, HEAD_DIM), jnp.int32)
    at = jnp.int32(0)
    for r in range(rows):
        length = lens[r]
        starts = jnp.where(row_id == r, at, starts)
        lengths = jnp.where(row_id == r, length, lengths)
        at = at + length
    ends = starts + lengths
    angles = lengths.astype(F32) * freq[0:1, :]
    cosine = jnp.cos(angles)
    sine = jnp.sin(angles)
    sine = jnp.where(lane < HEAD_DIM // 2, -sine, sine)

    yq_copy.wait_recv()
    sq[...] = pq[yi] + yq[...]
    zq_copies = []
    for d in range(1, m):
        t = lax.rem(zi + d, m)
        zq_copies.append(
            send(sq.at[t], zq.at[d - 1], rs_send.at[0, d], rs_recv.at[0, d], t * 2 + yi, hi)
        )
    ykv_copy.wait_recv()
    skv[...] = (pkv[yi].astype(F32) + ykv[...].astype(F32)).astype(BF16)
    zkv_copies = []
    for d in range(1, m):
        t = lax.rem(zi + d, m)
        zkv_copies.append(
            send(skv.at[t], zkv.at[d - 1], rs_send.at[1, d], rs_recv.at[1, d], t * 2 + yi, hi)
        )
    pending += zq_copies + zkv_copies
    loads[3].wait()
    wout_t[...] = wout[...].astype(F32).T.astype(BF16)
    query = sq[zi]
    for d in range(1, m):
        zq_copies[d - 1].wait_recv()
        query = query + zq[d - 1]

    def share_power(values, which):
        power = jnp.sum(values * values, axis=1, keepdims=True)
        sqs[which] = jnp.broadcast_to(power, (rows, HEAD_DIM))
        copies = []
        for d in range(1, heads_axis):
            copies.append(
                send(sqs.at[which], sqr.at[which, d - 1], sq_send.at[which, d - 1],
                     sq_recv.at[which, d - 1], me, lax.rem(hi + d, heads_axis))
            )
        pending.extend(copies)
        return copies

    def inverse_root(copies, which):
        power = sqs[which]
        for d in range(1, heads_axis):
            copies[d - 1].wait_recv()
            power = power + sqr[which, d - 1]
        return lax.rsqrt(power[:, 0:1] / (width * heads_axis) + EPS)

    def rotate(values):
        parts = []
        for h in range(heads):
            part = values[:, h * HEAD_DIM : (h + 1) * HEAD_DIM]
            parts.append(part * cosine + pltpu.roll(part, HEAD_DIM // 2, 1) * sine)
        return jnp.concatenate(parts, axis=1)

    q_copies = share_power(query, 0)
    query = query * qkg[0:1, :]
    query_rot = rotate(query * inverse_root(q_copies, 0)).astype(BF16).astype(F32)

    scale = HEAD_DIM ** (-0.5)
    wide_lane = lax.broadcasted_iota(jnp.int32, (rows, width), 1)
    q_rows = []
    for h in range(heads):
        inside = (wide_lane >= h * HEAD_DIM) & (wide_lane < (h + 1) * HEAD_DIM)
        q_rows.append(jnp.where(inside, query_rot, 0.0))
    q_cols = jnp.concatenate(q_rows, axis=0).T.astype(BF16)
    first = jnp.concatenate([starts[:, 0:1]] * heads, axis=0)
    last = jnp.concatenate([ends[:, 0:1]] * heads, axis=0)
    pool = ck.shape[0]
    loads[1].wait()
    highest = jnp.full((heads * rows, KEY_BLOCK), -1e30, F32)
    column = lax.broadcasted_iota(jnp.int32, (heads * rows, KEY_BLOCK), 1)
    for b in range(pool // KEY_BLOCK):
        span = pl.ds(b * KEY_BLOCK, KEY_BLOCK)
        s = dot(ck[span, :], q_cols).T * scale
        place = b * KEY_BLOCK + column
        s = jnp.where((place >= first) & (place < last), s, -1e30)
        scores[:, span] = s
        highest = jnp.maximum(highest, s)
    highest = jnp.max(highest, axis=1, keepdims=True)

    both = skv[zi].astype(F32)
    for d in range(1, m):
        zkv_copies[d - 1].wait_recv()
        both = both + zkv[d - 1].astype(F32)
    key_new = both[:, :width]
    value_new = both[:, width:].astype(BF16)
    nv[...] = value_new
    k_copies = share_power(key_new, 1)

    total = jnp.zeros((heads * rows, KEY_BLOCK), F32)
    numerator = jnp.zeros((heads * rows, width), F32)
    loads[2].wait()
    for b in range(pool // KEY_BLOCK):
        span = pl.ds(b * KEY_BLOCK, KEY_BLOCK)
        w = jnp.exp(scores[:, span] - highest).astype(BF16)
        total = total + w.astype(F32)
        numerator = numerator + dot(w, cv[span, :])
    denominator = jnp.sum(total, axis=1, keepdims=True)

    key_rot = rotate(key_new * inverse_root(k_copies, 1) * qkg[1:2, :]).astype(BF16)
    nk[...] = key_rot
    own = query_rot * key_rot.astype(F32)
    own = jnp.concatenate(
        [
            jnp.sum(own[:, h * HEAD_DIM : (h + 1) * HEAD_DIM], axis=1, keepdims=True)
            for h in range(heads)
        ],
        axis=0,
    ) * scale
    top = jnp.maximum(highest, own)
    factor = jnp.exp(highest - top)
    own_weight = jnp.exp(own - top).astype(BF16).astype(F32)
    denominator = denominator * factor + own_weight
    numerator = numerator * factor + own_weight * jnp.concatenate(
        [value_new.astype(F32)] * heads, axis=0
    )
    ratio = numerator / denominator
    attended = jnp.concatenate(
        [
            ratio[h * rows : (h + 1) * rows, h * HEAD_DIM : (h + 1) * HEAD_DIM]
            for h in range(heads)
        ],
        axis=1,
    ).astype(BF16)
    att[slot] = attended
    att_copies = []
    for d in range(1, n):
        t = lax.rem(me + d, n)
        att_copies.append(
            send(att.at[slot], att.at[slot], att_send.at[d - 1], att_recv.at[d - 1], t, hi)
        )
    pending += att_copies
    for d in range(1, n):
        s = lax.rem(me - d + n, n)
        there = att.at[lax.rem(s, 2) * m + lax.div(s, 2)]
        pltpu.make_async_remote_copy(
            src_ref=there, dst_ref=there, send_sem=att_send.at[d - 1],
            recv_sem=att_recv.at[d - 1], device_id=(s, hi), device_id_type=MESH,
        ).wait_recv()

    def sum_heads(part, which):
        bit = 1
        step = 0
        while bit < heads_axis:
            rounded = part.astype(BF16)
            ar_src[which, step] = rounded
            partner = hi + bit - 2 * bit * lax.rem(lax.div(hi, bit), 2)
            copy = send(ar_src.at[which, step], ar_dst.at[which, step],
                        ar_send.at[which, step], ar_recv.at[which, step], me, partner)
            pending.append(copy)
            copy.wait_recv()
            part = rounded.astype(F32) + ar_dst[which, step].astype(F32)
            bit *= 2
            step += 1
        return part

    eye = lax.broadcasted_iota(jnp.int32, (total_rows, total_rows), 0) == lax.broadcasted_iota(
        jnp.int32, (total_rows, total_rows), 1
    )

    def inverse_rms(part, which):
        power = jnp.sum(part * part, axis=1, keepdims=True)
        flat = jnp.sum(jnp.where(eye, power, 0.0), axis=0, keepdims=True)
        pw_src[which] = jnp.broadcast_to(flat, (8, total_rows))
        copies = []
        for d in range(1, n):
            copies.append(
                send(pw_src.at[which], pw_dst.at[which, d - 1], pw_send.at[which, d - 1],
                     pw_recv.at[which, d - 1], lax.rem(me + d, n), hi)
            )
        pending.extend(copies)
        for d in range(1, n):
            copies[d - 1].wait_recv()
            flat = flat + pw_dst[which, d - 1, 0:1, :]
        scaled = lax.rsqrt(flat / model_width + EPS)
        return jnp.sum(jnp.where(eye, scaled, 0.0), axis=1, keepdims=True)

    attn = sum_heads(dot(att[...].reshape(total_rows, width), wout_t[...]), 0)
    attn = attn * inverse_rms(attn, 0) * ng[0:1, :]
    hm[...] = (hp[...].astype(F32) + attn).astype(BF16)

    units = wgu.shape[2]
    cu = units // CHUNKS
    loads[4].wait()
    gy_copies = []
    for c in range(CHUNKS):
        cols = pl.ds(c * cu, cu)
        gp[c, :, :, :, :cu] = dot(hm[...], wgu[0, :, cols]).astype(BF16).reshape(2, m, rows, cu)
        gp[c, :, :, :, cu:] = dot(hm[...], wgu[1, :, cols]).astype(BF16).reshape(2, m, rows, cu)
        gy_copies.append(
            send(gp.at[c, 1 - yi], gy.at[c], gy_send.at[c], gy_recv.at[c], ypart, hi)
        )
    pending += gy_copies
    loads[5].wait()
    wdn_t[...] = wdn[...].astype(F32).T.astype(BF16)
    gz_copies = {}
    ay_copies = {}
    az_copies = {}
    state = {"down": None}

    def pair_sum(c):
        gy_copies[c].wait_recv()
        gs[c] = (gp[c, yi].astype(F32) + gy[c].astype(F32)).astype(BF16)
        for d in range(1, m):
            t = lax.rem(zi + d, m)
            gz_copies[c, d] = send(gs.at[c, t], gz.at[c, d - 1], gz_send.at[c, d - 1],
                                   gz_recv.at[c, d - 1], t * 2 + yi, hi)
            pending.append(gz_copies[c, d])

    def activate(c):
        full = gs[c, zi].astype(F32)
        for d in range(1, m):
            gz_copies[c, d].wait_recv()
            full = full + gz[c, d - 1].astype(F32)
        gate = full[:, :cu]
        act[c, slot] = (gate / (1.0 + jnp.exp(-gate)) * full[:, cu:]).astype(BF16)
        for d in range(1, m):
            t = lax.rem(zi + d, m)
            az_copies[c, d] = send(act.at[c, slot], act.at[c, slot], az_send.at[c, d - 1],
                                   az_recv.at[c, d - 1], t * 2 + yi, hi)
            pending.append(az_copies[c, d])

    def forward(c):
        for d in range(1, m):
            s = lax.rem(zi - d + m, m)
            there = act.at[c, yi * m + s]
            pltpu.make_async_remote_copy(
                src_ref=there, dst_ref=there, send_sem=az_send.at[c, d - 1],
                recv_sem=az_recv.at[c, d - 1], device_id=(s * 2 + yi, hi), device_id_type=MESH,
            ).wait_recv()
        mine = act.at[c, pl.ds(yi * m, m)]
        ay_copies[c] = send(mine, mine, ay_send.at[c], ay_recv.at[c], ypart, hi)
        pending.append(ay_copies[c])

    def project(c):
        other = act.at[c, pl.ds((1 - yi) * m, m)]
        pltpu.make_async_remote_copy(
            src_ref=other, dst_ref=other, send_sem=ay_send.at[c], recv_sem=ay_recv.at[c],
            device_id=(ypart, hi), device_id_type=MESH,
        ).wait_recv()
        part = dot(act[c].reshape(total_rows, cu), wdn_t[pl.ds(c * cu, cu), :])
        state["down"] = part if state["down"] is None else state["down"] + part

    stages = (pair_sum, activate, forward, project)
    for step in range(CHUNKS + len(stages) - 1):
        for k, stage in enumerate(stages):
            if 0 <= step - k < CHUNKS:
                stage(step - k)
    ffn = sum_heads(state["down"], 1)
    ffn = ffn * inverse_rms(ffn, 1) * ng[1:2, :]
    result = (hm[...].astype(F32) + ffn).astype(BF16)
    for y in range(2):
        for z in range(m):
            p = (y * m + z) * rows
            out[pl.ds((z * 2 + y) * rows, rows), :] = result[p : p + rows]
    for copy in pending:
        copy.wait_send()


def body(
    n, heads_axis,
    hidden_in, lengths, w_qkv, qk_gain, cache_keys, cache_values,
    w_out, norm_gain, w_gate_up, w_down,
):
    rows = lengths.shape[0]
    total_rows, feat = hidden_in.shape
    width = w_qkv.shape[2]
    heads = width // HEAD_DIM
    units = w_gate_up.shape[2]
    m = n // 2
    cu = units // CHUNKS
    half = HEAD_DIM // 2
    steps = max(1, heads_axis.bit_length() - 1)
    freqs = np.power(THETA, -(np.arange(half, dtype=np.float64) * 2.0 / HEAD_DIM))
    freqs = np.broadcast_to(np.concatenate([freqs, freqs]), (8, HEAD_DIM)).astype(np.float32)
    dma = pltpu.SemaphoreType.DMA
    vmem = pltpu.VMEM
    scratch = [
        vmem(w_qkv.shape, BF16), vmem(cache_keys.shape, BF16), vmem(cache_values.shape, BF16),
        vmem(w_out.shape, BF16), vmem(w_gate_up.shape, BF16), vmem(w_down.shape, BF16),
        vmem(w_out.shape[::-1], BF16), vmem(w_down.shape[::-1], BF16), dma((6,)),
        vmem((total_rows, feat), BF16),
        vmem((2, m, rows, width), F32), vmem((m, rows, width), F32),
        vmem((m, rows, width), F32), vmem((m - 1, rows, width), F32),
        vmem((2, m, rows, 2 * width), BF16), vmem((m, rows, 2 * width), BF16),
        vmem((m, rows, 2 * width), BF16), vmem((m - 1, rows, 2 * width), BF16),
        dma((2, m)), dma((2, m)),
        vmem((2, rows, HEAD_DIM), F32), vmem((2, heads_axis - 1, rows, HEAD_DIM), F32),
        dma((2, heads_axis - 1)), dma((2, heads_axis - 1)),
        vmem((heads * rows, cache_keys.shape[0]), F32),
        vmem((n, rows, width), BF16), dma((n - 1,)), dma((n - 1,)),
        vmem((2, steps, total_rows, feat), BF16), vmem((2, steps, total_rows, feat), BF16),
        dma((2, steps)), dma((2, steps)),
        vmem((2, 8, total_rows), F32), vmem((2, n - 1, 8, total_rows), F32),
        dma((2, n - 1)), dma((2, n - 1)),
        vmem((total_rows, feat), BF16),
        vmem((CHUNKS, 2, m, rows, 2 * cu), BF16), vmem((CHUNKS, m, rows, 2 * cu), BF16),
        vmem((CHUNKS, m, rows, 2 * cu), BF16), vmem((CHUNKS, m - 1, rows, 2 * cu), BF16),
        dma((CHUNKS,)), dma((CHUNKS,)), dma((CHUNKS, m - 1)), dma((CHUNKS, m - 1)),
        vmem((CHUNKS, n, rows, cu), BF16),
        dma((CHUNKS, m - 1)), dma((CHUNKS, m - 1)), dma((CHUNKS,)), dma((CHUNKS,)),
    ]
    in_vmem = pl.BlockSpec(memory_space=pltpu.VMEM)
    anywhere = pl.BlockSpec(memory_space=pl.ANY)
    in_hbm = pl.BlockSpec(memory_space=pltpu.HBM)
    outs = pl.pallas_call(
        functools.partial(kernel, n, heads_axis, feat * n),
        out_shape=(
            jax.ShapeDtypeStruct((total_rows, feat), BF16),
            jax.ShapeDtypeStruct((rows, width), BF16),
            jax.ShapeDtypeStruct((rows, width), BF16),
        ),
        in_specs=[pl.BlockSpec(memory_space=pltpu.SMEM)] + [in_vmem] * 4 + [anywhere] * 6,
        out_specs=(in_vmem,) * 3,
        scratch_shapes=scratch,
        compiler_params=pltpu.CompilerParams(
            collective_id=0, has_side_effects=True, vmem_limit_bytes=56 * 1024 * 1024
        ),
    )(
        lengths, hidden_in, qk_gain, norm_gain, jnp.asarray(freqs),
        w_qkv, cache_keys, cache_values, w_out, w_gate_up, w_down,
    )
    return pl.pallas_call(
        place_outputs,
        out_shape=tuple(jax.ShapeDtypeStruct(a.shape, a.dtype) for a in outs),
        in_specs=[in_hbm] * 3,
        out_specs=(in_hbm,) * 3,
        scratch_shapes=[dma((3,))],
    )(*outs)


def solution(mesh):
    return jax.shard_map(
        functools.partial(body, mesh.shape["req"], mesh.shape["head"]),
        mesh=mesh,
        in_specs=(
            P(None, "req"),
            P("req"),
            P(None, "req", "head"),
            P(None, "head"),
            P("req", "head"),
            P("req", "head"),
            P("req", "head"),
            P(None, "req"),
            P(None, "req", "head"),
            P("req", "head"),
        ),
        out_specs=(P(None, "req"), P("req", "head"), P("req", "head")),
        check_vma=False,
    )
```

```python
import functools

import jax
import jax.numpy as jnp
import numpy as np
from jax import lax
from jax.experimental import pallas as pl
from jax.experimental.pallas import tpu as pltpu
from jax.sharding import PartitionSpec as P

HEAD_DIM = 128
EPS = 1e-06
THETA = 500000.0
MESH = pl.DeviceIdType.MESH
F32 = jnp.float32
BF16 = jnp.bfloat16
CHUNKS = 4
KEY_BLOCK = 512


def dot(left, right):
    return lax.dot_general(left, right, (((1,), (0,)), ((), ())), preferred_element_type=F32)


def place_outputs(a, b, c, out_a, out_b, out_c):
    out_a[...] = a[...]
    out_b[...] = b[...]
    out_c[...] = c[...]


def kernel(
    n, heads_axis, model_width,
    lens, hid_h, qkg_h, ng_h, freq_h, wqkv_h, ck_h, cv_h, wout_h, wgu_h, wdn_h,
    out, nk, nv,
    wqkv, ck, cv, wout, wgu, wdn, wout_t, wdn_t, load_sem,
    hid, qkg, ng, freq, small_sem,
    hp, pq, zq, pkv, zkv, rs_send, rs_recv,
    sqs, sqr, sq_send, sq_recv,
    scores, att, att_send, att_recv,
    ar, ar_send, ar_recv,
    pw_src, pw_dst, pw_send, pw_recv,
    hm, gp, gy, gs, gz, gy_send, gy_recv, gz_send, gz_recv,
    act, az_send, az_recv, ay_send, ay_recv,
):
    me = lax.axis_index("req")
    hi = lax.axis_index("head")
    m = n // 2
    zi = lax.div(me, 2)
    yi = lax.rem(me, 2)
    rows = lens.shape[0]
    width = qkg.shape[1]
    heads = width // HEAD_DIM
    total_rows = n * rows
    slot = yi * m + zi
    ypart = zi * 2 + (1 - yi)

    def loader(index, src, dst):
        return pltpu.make_async_copy(src, dst, load_sem.at[index])

    loads = [
        loader(0, wqkv_h, wqkv), loader(1, ck_h, ck), loader(2, cv_h, cv),
        loader(3, wout_h, wout), loader(4, wgu_h, wgu), loader(5, wdn_h, wdn),
    ]
    small_loads = [
        pltpu.make_async_copy(src, dst, small_sem.at[i])
        for i, (src, dst) in enumerate(((hid_h, hid), (qkg_h, qkg), (ng_h, ng), (freq_h, freq)))
    ]
    small_loads[0].start()
    loads[0].start()
    for load in small_loads[1:]:
        load.start()

    barrier = pltpu.get_barrier_semaphore()
    for d in range(1, n):
        pl.semaphore_signal(barrier, inc=1, device_id=(lax.rem(me + d, n), hi), device_id_type=MESH)
    for d in range(1, heads_axis):
        pl.semaphore_signal(
            barrier, inc=1, device_id=(me, lax.rem(hi + d, heads_axis)), device_id_type=MESH
        )

    def send(src, dst, ssem, rsem, req, head):
        copy = pltpu.make_async_remote_copy(
            src_ref=src, dst_ref=dst, send_sem=ssem, recv_sem=rsem,
            device_id=(req, head), device_id_type=MESH,
        )
        copy.start()
        return copy

    pending = []

    small_loads[0].wait()
    for y in range(2):
        for z in range(m):
            hp[pl.ds((y * m + z) * rows, rows), :] = hid[pl.ds((z * 2 + y) * rows, rows), :]
    loads[0].wait()
    for load in loads[1:]:
        load.start()
    x = hp[...]
    pq[...] = dot(x, wqkv[0]).astype(BF16).reshape(n, rows, width)
    pl.semaphore_wait(barrier, n - 1 + heads_axis - 1)

    def scatter(src, dst, which):
        copies = []
        for d in range(1, n):
            t = lax.rem(me + d, n)
            place = lax.rem(t, 2) * m + lax.div(t, 2)
            copies.append(
                send(src.at[place], dst.at[d - 1], rs_send.at[which, d - 1],
                     rs_recv.at[which, d - 1], t, hi)
            )
        pending.extend(copies)
        return copies

    def gathered(src, dst, copies):
        total = src[slot].astype(F32)
        for d in range(1, n):
            copies[d - 1].wait_recv()
            total = total + dst[d - 1].astype(F32)
        return total

    zq_copies = scatter(pq, zq, 0)
    pkv[:, :, :width] = dot(x, wqkv[1]).astype(BF16).reshape(n, rows, width)
    pkv[:, :, width:] = dot(x, wqkv[2]).astype(BF16).reshape(n, rows, width)
    zkv_copies = scatter(pkv, zkv, 1)

    row_id = lax.broadcasted_iota(jnp.int32, (rows, HEAD_DIM), 0)
    lane = lax.broadcasted_iota(jnp.int32, (rows, HEAD_DIM), 1)
    starts = jnp.zeros((rows, HEAD_DIM), jnp.int32)
    lengths = jnp.zeros((rows, HEAD_DIM), jnp.int32)
    at = jnp.int32(0)
    for r in range(rows):
        length = lens[r]
        starts = jnp.where(row_id == r, at, starts)
        lengths = jnp.where(row_id == r, length, lengths)
        at = at + length
    ends = starts + lengths
    small_loads[3].wait()
    angles = lengths.astype(F32) * freq[0:1, :]
    cosine = jnp.cos(angles)
    sine = jnp.sin(angles)
    sine = jnp.where(lane < HEAD_DIM // 2, -sine, sine)

    loads[3].wait()
    wout_t[...] = wout[...].astype(F32).T.astype(BF16)
    small_loads[1].wait()
    query = gathered(pq, zq, zq_copies)

    def share_power(values, which):
        power = jnp.sum(values * values, axis=1, keepdims=True)
        sqs[which] = jnp.broadcast_to(power, (rows, HEAD_DIM))
        copies = []
        for d in range(1, heads_axis):
            copies.append(
                send(sqs.at[which], sqr.at[which, d - 1], sq_send.at[which, d - 1],
                     sq_recv.at[which, d - 1], me, lax.rem(hi + d, heads_axis))
            )
        pending.extend(copies)
        return copies

    def inverse_root(copies, which):
        power = sqs[which]
        for d in range(1, heads_axis):
            copies[d - 1].wait_recv()
            power = power + sqr[which, d - 1]
        return lax.rsqrt(power[:, 0:1] / (width * heads_axis) + EPS)

    def rotate(values):
        parts = []
        for h in range(heads):
            part = values[:, h * HEAD_DIM : (h + 1) * HEAD_DIM]
            parts.append(part * cosine + pltpu.roll(part, HEAD_DIM // 2, 1) * sine)
        return jnp.concatenate(parts, axis=1)

    q_copies = share_power(query, 0)
    query_rot = rotate(query * qkg[0:1, :]).astype(BF16).astype(F32)

    scale = HEAD_DIM ** (-0.5)
    wide_lane = lax.broadcasted_iota(jnp.int32, (rows, width), 1)
    q_rows = []
    for h in range(heads):
        inside = (wide_lane >= h * HEAD_DIM) & (wide_lane < (h + 1) * HEAD_DIM)
        q_rows.append(jnp.where(inside, query_rot, 0.0))
    q_cols = jnp.concatenate(q_rows, axis=0).T.astype(BF16)
    first = jnp.concatenate([starts[:, 0:1]] * heads, axis=0)
    last = jnp.concatenate([ends[:, 0:1]] * heads, axis=0)
    pool = ck.shape[0]
    loads[1].wait()
    q_scale = jnp.concatenate([inverse_root(q_copies, 0) * scale] * heads, axis=0)
    highest = jnp.full((heads * rows, KEY_BLOCK), -1e30, F32)
    column = lax.broadcasted_iota(jnp.int32, (heads * rows, KEY_BLOCK), 1)
    for b in range(pool // KEY_BLOCK):
        span = pl.ds(b * KEY_BLOCK, KEY_BLOCK)
        s = dot(ck[span, :], q_cols).T * q_scale
        place = b * KEY_BLOCK + column
        s = jnp.where((place >= first) & (place < last), s, -1e30)
        scores[:, span] = s
        highest = jnp.maximum(highest, s)
    highest = jnp.max(highest, axis=1, keepdims=True)

    both = gathered(pkv, zkv, zkv_copies)
    key_new = both[:, :width]
    value_new = both[:, width:].astype(BF16)
    nv[...] = value_new
    k_copies = share_power(key_new, 1)

    total = jnp.zeros((heads * rows, KEY_BLOCK), F32)
    numerator = jnp.zeros((heads * rows, width), F32)
    loads[2].wait()
    for b in range(pool // KEY_BLOCK):
        span = pl.ds(b * KEY_BLOCK, KEY_BLOCK)
        w = jnp.exp(scores[:, span] - highest).astype(BF16)
        total = total + w.astype(F32)
        numerator = numerator + dot(w, cv[span, :])
    denominator = jnp.sum(total, axis=1, keepdims=True)

    key_rot = rotate(key_new * inverse_root(k_copies, 1) * qkg[1:2, :]).astype(BF16)
    nk[...] = key_rot
    own = query_rot * key_rot.astype(F32)
    own = jnp.concatenate(
        [
            jnp.sum(own[:, h * HEAD_DIM : (h + 1) * HEAD_DIM], axis=1, keepdims=True)
            for h in range(heads)
        ],
        axis=0,
    ) * q_scale
    top = jnp.maximum(highest, own)
    factor = jnp.exp(highest - top)
    own_weight = jnp.exp(own - top).astype(BF16).astype(F32)
    denominator = denominator * factor + own_weight
    numerator = numerator * factor + own_weight * jnp.concatenate(
        [value_new.astype(F32)] * heads, axis=0
    )
    ratio = numerator / denominator
    attended = jnp.concatenate(
        [
            ratio[h * rows : (h + 1) * rows, h * HEAD_DIM : (h + 1) * HEAD_DIM]
            for h in range(heads)
        ],
        axis=1,
    ).astype(BF16)
    att[slot] = attended
    att_copies = []
    for d in range(1, n):
        t = lax.rem(me + d, n)
        att_copies.append(
            send(att.at[slot], att.at[slot], att_send.at[d - 1], att_recv.at[d - 1], t, hi)
        )
    pending += att_copies
    for d in range(1, n):
        s = lax.rem(me - d + n, n)
        there = att.at[lax.rem(s, 2) * m + lax.div(s, 2)]
        pltpu.make_async_remote_copy(
            src_ref=there, dst_ref=there, send_sem=att_send.at[d - 1],
            recv_sem=att_recv.at[d - 1], device_id=(s, hi), device_id_type=MESH,
        ).wait_recv()

    def sum_heads(part, which):
        held = ar.at[which]
        held[hi] = part.astype(BF16)
        copies = []
        for d in range(1, heads_axis):
            copies.append(
                send(held.at[hi], held.at[hi], ar_send.at[which, d - 1],
                     ar_recv.at[which, d - 1], me, lax.rem(hi + d, heads_axis))
            )
        pending.extend(copies)
        for d in range(1, heads_axis):
            there = held.at[lax.rem(hi - d + heads_axis, heads_axis)]
            pltpu.make_async_remote_copy(
                src_ref=there, dst_ref=there, send_sem=ar_send.at[which, d - 1],
                recv_sem=ar_recv.at[which, d - 1],
                device_id=(me, lax.rem(hi - d + heads_axis, heads_axis)), device_id_type=MESH,
            ).wait_recv()
        whole = held[0].astype(F32)
        for h in range(1, heads_axis):
            whole = whole + held[h].astype(F32)
        return whole

    eye = lax.broadcasted_iota(jnp.int32, (total_rows, total_rows), 0) == lax.broadcasted_iota(
        jnp.int32, (total_rows, total_rows), 1
    )

    def inverse_rms(part, which):
        power = jnp.sum(part * part, axis=1, keepdims=True)
        flat = jnp.sum(jnp.where(eye, power, 0.0), axis=0, keepdims=True)
        pw_src[which] = jnp.broadcast_to(flat, (8, total_rows))
        copies = []
        for d in range(1, n):
            copies.append(
                send(pw_src.at[which], pw_dst.at[which, d - 1], pw_send.at[which, d - 1],
                     pw_recv.at[which, d - 1], lax.rem(me + d, n), hi)
            )
        pending.extend(copies)
        for d in range(1, n):
            copies[d - 1].wait_recv()
            flat = flat + pw_dst[which, d - 1, 0:1, :]
        scaled = lax.rsqrt(flat / model_width + EPS)
        return jnp.sum(jnp.where(eye, scaled, 0.0), axis=1, keepdims=True)

    small_loads[2].wait()
    attn = sum_heads(dot(att[...].reshape(total_rows, width), wout_t[...]), 0)
    attn = attn * inverse_rms(attn, 0) * ng[0:1, :]
    hm[...] = (hp[...].astype(F32) + attn).astype(BF16)

    units = wgu.shape[2]
    cu = units // CHUNKS
    loads[4].wait()
    gy_copies = []
    for c in range(CHUNKS):
        cols = pl.ds(c * cu, cu)
        gp[c, :, :, :, :cu] = dot(hm[...], wgu[0, :, cols]).astype(BF16).reshape(2, m, rows, cu)
        gp[c, :, :, :, cu:] = dot(hm[...], wgu[1, :, cols]).astype(BF16).reshape(2, m, rows, cu)
        gy_copies.append(
            send(gp.at[c, 1 - yi], gy.at[c], gy_send.at[c], gy_recv.at[c], ypart, hi)
        )
    pending += gy_copies
    loads[5].wait()
    wdn_t[...] = wdn[...].astype(F32).T.astype(BF16)
    gz_copies = {}
    ay_copies = {}
    az_copies = {}
    state = {"down": None}

    def pair_sum(c):
        gy_copies[c].wait_recv()
        gs[c] = (gp[c, yi].astype(F32) + gy[c].astype(F32)).astype(BF16)
        for d in range(1, m):
            t = lax.rem(zi + d, m)
            gz_copies[c, d] = send(gs.at[c, t], gz.at[c, d - 1], gz_send.at[c, d - 1],
                                   gz_recv.at[c, d - 1], t * 2 + yi, hi)
            pending.append(gz_copies[c, d])

    def activate(c):
        full = gs[c, zi].astype(F32)
        for d in range(1, m):
            gz_copies[c, d].wait_recv()
            full = full + gz[c, d - 1].astype(F32)
        gate = full[:, :cu]
        act[c, slot] = (gate / (1.0 + jnp.exp(-gate)) * full[:, cu:]).astype(BF16)
        for d in range(1, m):
            t = lax.rem(zi + d, m)
            az_copies[c, d] = send(act.at[c, slot], act.at[c, slot], az_send.at[c, d - 1],
                                   az_recv.at[c, d - 1], t * 2 + yi, hi)
            pending.append(az_copies[c, d])

    def forward(c):
        for d in range(1, m):
            s = lax.rem(zi - d + m, m)
            there = act.at[c, yi * m + s]
            pltpu.make_async_remote_copy(
                src_ref=there, dst_ref=there, send_sem=az_send.at[c, d - 1],
                recv_sem=az_recv.at[c, d - 1], device_id=(s * 2 + yi, hi), device_id_type=MESH,
            ).wait_recv()
        mine = act.at[c, pl.ds(yi * m, m)]
        ay_copies[c] = send(mine, mine, ay_send.at[c], ay_recv.at[c], ypart, hi)
        pending.append(ay_copies[c])

    def project(c):
        other = act.at[c, pl.ds((1 - yi) * m, m)]
        pltpu.make_async_remote_copy(
            src_ref=other, dst_ref=other, send_sem=ay_send.at[c], recv_sem=ay_recv.at[c],
            device_id=(ypart, hi), device_id_type=MESH,
        ).wait_recv()
        part = dot(act[c].reshape(total_rows, cu), wdn_t[pl.ds(c * cu, cu), :])
        state["down"] = part if state["down"] is None else state["down"] + part

    stages = (pair_sum, activate, forward, project)
    for step in range(CHUNKS + len(stages) - 1):
        for k, stage in enumerate(stages):
            if 0 <= step - k < CHUNKS:
                stage(step - k)
    ffn = sum_heads(state["down"], 1)
    ffn = ffn * inverse_rms(ffn, 1) * ng[1:2, :]
    result = (hm[...].astype(F32) + ffn).astype(BF16)
    for y in range(2):
        for z in range(m):
            p = (y * m + z) * rows
            out[pl.ds((z * 2 + y) * rows, rows), :] = result[p : p + rows]
    for copy in pending:
        copy.wait_send()


def body(
    n, heads_axis,
    hidden_in, lengths, w_qkv, qk_gain, cache_keys, cache_values,
    w_out, norm_gain, w_gate_up, w_down,
):
    rows = lengths.shape[0]
    total_rows, feat = hidden_in.shape
    width = w_qkv.shape[2]
    heads = width // HEAD_DIM
    units = w_gate_up.shape[2]
    m = n // 2
    cu = units // CHUNKS
    half = HEAD_DIM // 2
    freqs = np.power(THETA, -(np.arange(half, dtype=np.float64) * 2.0 / HEAD_DIM))
    freqs = np.broadcast_to(np.concatenate([freqs, freqs]), (8, HEAD_DIM)).astype(np.float32)
    dma = pltpu.SemaphoreType.DMA
    vmem = pltpu.VMEM
    scratch = [
        vmem(w_qkv.shape, BF16), vmem(cache_keys.shape, BF16), vmem(cache_values.shape, BF16),
        vmem(w_out.shape, BF16), vmem(w_gate_up.shape, BF16), vmem(w_down.shape, BF16),
        vmem(w_out.shape[::-1], BF16), vmem(w_down.shape[::-1], BF16), dma((6,)),
        vmem(hidden_in.shape, BF16), vmem(qk_gain.shape, F32), vmem(norm_gain.shape, F32),
        vmem((8, HEAD_DIM), F32), dma((4,)),
        vmem((total_rows, feat), BF16),
        vmem((n, rows, width), BF16), vmem((n - 1, rows, width), BF16),
        vmem((n, rows, 2 * width), BF16), vmem((n - 1, rows, 2 * width), BF16),
        dma((2, n - 1)), dma((2, n - 1)),
        vmem((2, rows, HEAD_DIM), F32), vmem((2, heads_axis - 1, rows, HEAD_DIM), F32),
        dma((2, heads_axis - 1)), dma((2, heads_axis - 1)),
        vmem((heads * rows, cache_keys.shape[0]), F32),
        vmem((n, rows, width), BF16), dma((n - 1,)), dma((n - 1,)),
        vmem((2, heads_axis, total_rows, feat), BF16),
        dma((2, heads_axis - 1)), dma((2, heads_axis - 1)),
        vmem((2, 8, total_rows), F32), vmem((2, n - 1, 8, total_rows), F32),
        dma((2, n - 1)), dma((2, n - 1)),
        vmem((total_rows, feat), BF16),
        vmem((CHUNKS, 2, m, rows, 2 * cu), BF16), vmem((CHUNKS, m, rows, 2 * cu), BF16),
        vmem((CHUNKS, m, rows, 2 * cu), BF16), vmem((CHUNKS, m - 1, rows, 2 * cu), BF16),
        dma((CHUNKS,)), dma((CHUNKS,)), dma((CHUNKS, m - 1)), dma((CHUNKS, m - 1)),
        vmem((CHUNKS, n, rows, cu), BF16),
        dma((CHUNKS, m - 1)), dma((CHUNKS, m - 1)), dma((CHUNKS,)), dma((CHUNKS,)),
    ]
    in_vmem = pl.BlockSpec(memory_space=pltpu.VMEM)
    anywhere = pl.BlockSpec(memory_space=pl.ANY)
    outs = pl.pallas_call(
        functools.partial(kernel, n, heads_axis, feat * n),
        out_shape=(
            jax.ShapeDtypeStruct((total_rows, feat), BF16),
            jax.ShapeDtypeStruct((rows, width), BF16),
            jax.ShapeDtypeStruct((rows, width), BF16),
        ),
        in_specs=[pl.BlockSpec(memory_space=pltpu.SMEM)] + [anywhere] * 10,
        out_specs=(in_vmem,) * 3,
        scratch_shapes=scratch,
        compiler_params=pltpu.CompilerParams(
            collective_id=0, has_side_effects=True, vmem_limit_bytes=56 * 1024 * 1024
        ),
    )(
        lengths, hidden_in, qk_gain, norm_gain, jnp.asarray(freqs),
        w_qkv, cache_keys, cache_values, w_out, w_gate_up, w_down,
    )
    return pl.pallas_call(
        place_outputs,
        out_shape=tuple(jax.ShapeDtypeStruct(a.shape, a.dtype) for a in outs),
        in_specs=[in_vmem] * 3,
        out_specs=(in_vmem,) * 3,
    )(*outs)


def solution(mesh):
    return jax.shard_map(
        functools.partial(body, mesh.shape["req"], mesh.shape["head"]),
        mesh=mesh,
        in_specs=(
            P(None, "req"),
            P("req"),
            P(None, "req", "head"),
            P(None, "head"),
            P("req", "head"),
            P("req", "head"),
            P("req", "head"),
            P(None, "req"),
            P(None, "req", "head"),
            P("req", "head"),
        ),
        out_specs=(P(None, "req"), P("req", "head"), P("req", "head")),
        check_vma=False,
    )
```

```python
import functools

import jax
import jax.numpy as jnp
import numpy as np
from jax import lax
from jax.experimental import pallas as pl
from jax.experimental.pallas import tpu as pltpu
from jax.sharding import PartitionSpec as P

HEAD_DIM = 128
EPS = 1e-06
THETA = 500000.0
MESH = pl.DeviceIdType.MESH
F32 = jnp.float32
BF16 = jnp.bfloat16
CHUNKS = 8
KEY_BLOCK = 512


def dot(left, right):
    return lax.dot_general(left, right, (((1,), (0,)), ((), ())), preferred_element_type=F32)


def place_outputs(a, b, c, out_a, out_b, out_c):
    out_a[...] = a[...]
    out_b[...] = b[...]
    out_c[...] = c[...]


def kernel(
    n, heads_axis, model_width,
    lens, hid_h, qkg_h, ng_h, freq_h, wqkv_h, ck_h, cv_h, wout_h, wgu_h, wdn_h,
    out, nk, nv,
    wqkv, ck, cv, wout, wgu, wdn, wout_t, wdn_t, load_sem,
    hid, qkg, ng, freq, small_sem,
    hp, pq, zq, pk, zk, pv, zv, rs_send, rs_recv,
    sqs, sqr, sq_send, sq_recv,
    scores, att, att_send, att_recv,
    ar, ar_send, ar_recv,
    pw_src, pw_dst, pw_send, pw_recv,
    hm, gp, gy, gs, gz, gy_send, gy_recv, gz_send, gz_recv,
    act, az_send, az_recv, ay_send, ay_recv,
):
    me = lax.axis_index("req")
    hi = lax.axis_index("head")
    m = n // 2
    zi = lax.div(me, 2)
    yi = lax.rem(me, 2)
    rows = lens.shape[0]
    width = qkg.shape[1]
    heads = width // HEAD_DIM
    total_rows = n * rows
    slot = yi * m + zi
    ypart = zi * 2 + (1 - yi)

    def loader(index, src, dst):
        return pltpu.make_async_copy(src, dst, load_sem.at[index])

    loads = [
        loader(0, wqkv_h, wqkv), loader(1, ck_h, ck), loader(2, cv_h, cv),
        loader(3, wout_h, wout), loader(4, wgu_h, wgu), loader(5, wdn_h, wdn),
    ]
    small_loads = [
        pltpu.make_async_copy(src, dst, small_sem.at[i])
        for i, (src, dst) in enumerate(((hid_h, hid), (qkg_h, qkg), (ng_h, ng), (freq_h, freq)))
    ]
    small_loads[0].start()
    loads[0].start()
    for load in small_loads[1:]:
        load.start()

    barrier = pltpu.get_barrier_semaphore()
    for d in range(1, n):
        pl.semaphore_signal(barrier, inc=1, device_id=(lax.rem(me + d, n), hi), device_id_type=MESH)
    for d in range(1, heads_axis):
        pl.semaphore_signal(
            barrier, inc=1, device_id=(me, lax.rem(hi + d, heads_axis)), device_id_type=MESH
        )

    def send(src, dst, ssem, rsem, req, head):
        copy = pltpu.make_async_remote_copy(
            src_ref=src, dst_ref=dst, send_sem=ssem, recv_sem=rsem,
            device_id=(req, head), device_id_type=MESH,
        )
        copy.start()
        return copy

    pending = []

    small_loads[0].wait()
    for y in range(2):
        for z in range(m):
            hp[pl.ds((y * m + z) * rows, rows), :] = hid[pl.ds((z * 2 + y) * rows, rows), :]
    loads[0].wait()
    for load in loads[1:]:
        load.start()
    x = hp[...]
    pq[...] = dot(x, wqkv[0]).astype(BF16).reshape(n, rows, width)
    pl.semaphore_wait(barrier, n - 1 + heads_axis - 1)

    def scatter(src, dst, which):
        copies = []
        for d in range(1, n):
            t = lax.rem(me + d, n)
            place = lax.rem(t, 2) * m + lax.div(t, 2)
            copies.append(
                send(src.at[place], dst.at[d - 1], rs_send.at[which, d - 1],
                     rs_recv.at[which, d - 1], t, hi)
            )
        pending.extend(copies)
        return copies

    def gathered(src, dst, copies):
        total = src[slot].astype(F32)
        for d in range(1, n):
            copies[d - 1].wait_recv()
            total = total + dst[d - 1].astype(F32)
        return total

    zq_copies = scatter(pq, zq, 0)
    pk[...] = dot(x, wqkv[1]).astype(BF16).reshape(n, rows, width)
    zk_copies = scatter(pk, zk, 1)
    pv[...] = dot(x, wqkv[2]).astype(BF16).reshape(n, rows, width)
    zv_copies = scatter(pv, zv, 2)

    row_id = lax.broadcasted_iota(jnp.int32, (rows, HEAD_DIM), 0)
    lane = lax.broadcasted_iota(jnp.int32, (rows, HEAD_DIM), 1)
    starts = jnp.zeros((rows, HEAD_DIM), jnp.int32)
    lengths = jnp.zeros((rows, HEAD_DIM), jnp.int32)
    at = jnp.int32(0)
    for r in range(rows):
        length = lens[r]
        starts = jnp.where(row_id == r, at, starts)
        lengths = jnp.where(row_id == r, length, lengths)
        at = at + length
    ends = starts + lengths
    small_loads[3].wait()
    angles = lengths.astype(F32) * freq[0:1, :]
    cosine = jnp.cos(angles)
    sine = jnp.sin(angles)
    sine = jnp.where(lane < HEAD_DIM // 2, -sine, sine)

    loads[3].wait()
    wout_t[...] = wout[...].astype(F32).T.astype(BF16)
    small_loads[1].wait()
    query = gathered(pq, zq, zq_copies)

    def share_power(values, which):
        power = jnp.sum(values * values, axis=1, keepdims=True)
        sqs[which] = jnp.broadcast_to(power, (rows, HEAD_DIM))
        copies = []
        for d in range(1, heads_axis):
            copies.append(
                send(sqs.at[which], sqr.at[which, d - 1], sq_send.at[which, d - 1],
                     sq_recv.at[which, d - 1], me, lax.rem(hi + d, heads_axis))
            )
        pending.extend(copies)
        return copies

    def inverse_root(copies, which):
        power = sqs[which]
        for d in range(1, heads_axis):
            copies[d - 1].wait_recv()
            power = power + sqr[which, d - 1]
        return lax.rsqrt(power[:, 0:1] / (width * heads_axis) + EPS)

    def rotate(values):
        parts = []
        for h in range(heads):
            part = values[:, h * HEAD_DIM : (h + 1) * HEAD_DIM]
            parts.append(part * cosine + pltpu.roll(part, HEAD_DIM // 2, 1) * sine)
        return jnp.concatenate(parts, axis=1)

    q_copies = share_power(query, 0)
    query_rot = rotate(query * qkg[0:1, :]).astype(BF16).astype(F32)

    scale = HEAD_DIM ** (-0.5)
    wide_lane = lax.broadcasted_iota(jnp.int32, (rows, width), 1)
    q_rows = []
    for h in range(heads):
        inside = (wide_lane >= h * HEAD_DIM) & (wide_lane < (h + 1) * HEAD_DIM)
        q_rows.append(jnp.where(inside, query_rot, 0.0))
    q_cols = jnp.concatenate(q_rows, axis=0).T.astype(BF16)
    first = jnp.concatenate([starts[:, 0:1]] * heads, axis=0)
    last = jnp.concatenate([ends[:, 0:1]] * heads, axis=0)
    pool = ck.shape[0]
    loads[1].wait()
    q_scale = jnp.concatenate([inverse_root(q_copies, 0) * scale] * heads, axis=0)
    highest = jnp.full((heads * rows, KEY_BLOCK), -1e30, F32)
    column = lax.broadcasted_iota(jnp.int32, (heads * rows, KEY_BLOCK), 1)
    for b in range(pool // KEY_BLOCK):
        span = pl.ds(b * KEY_BLOCK, KEY_BLOCK)
        s = dot(ck[span, :], q_cols).T * q_scale
        place = b * KEY_BLOCK + column
        s = jnp.where((place >= first) & (place < last), s, -1e30)
        scores[:, span] = s
        highest = jnp.maximum(highest, s)
    highest = jnp.max(highest, axis=1, keepdims=True)

    key_new = gathered(pk, zk, zk_copies)
    k_copies = share_power(key_new, 1)

    total = jnp.zeros((heads * rows, KEY_BLOCK), F32)
    numerator = jnp.zeros((heads * rows, width), F32)
    loads[2].wait()
    for b in range(pool // KEY_BLOCK):
        span = pl.ds(b * KEY_BLOCK, KEY_BLOCK)
        w = jnp.exp(scores[:, span] - highest).astype(BF16)
        total = total + w.astype(F32)
        numerator = numerator + dot(w, cv[span, :])
    denominator = jnp.sum(total, axis=1, keepdims=True)

    value_new = gathered(pv, zv, zv_copies).astype(BF16)
    nv[...] = value_new
    key_rot = rotate(key_new * inverse_root(k_copies, 1) * qkg[1:2, :]).astype(BF16)
    nk[...] = key_rot
    own = query_rot * key_rot.astype(F32)
    own = jnp.concatenate(
        [
            jnp.sum(own[:, h * HEAD_DIM : (h + 1) * HEAD_DIM], axis=1, keepdims=True)
            for h in range(heads)
        ],
        axis=0,
    ) * q_scale
    top = jnp.maximum(highest, own)
    factor = jnp.exp(highest - top)
    own_weight = jnp.exp(own - top).astype(BF16).astype(F32)
    denominator = denominator * factor + own_weight
    numerator = numerator * factor + own_weight * jnp.concatenate(
        [value_new.astype(F32)] * heads, axis=0
    )
    ratio = numerator / denominator
    attended = jnp.concatenate(
        [
            ratio[h * rows : (h + 1) * rows, h * HEAD_DIM : (h + 1) * HEAD_DIM]
            for h in range(heads)
        ],
        axis=1,
    ).astype(BF16)
    att[slot] = attended
    att_copies = []
    for d in range(1, n):
        t = lax.rem(me + d, n)
        att_copies.append(
            send(att.at[slot], att.at[slot], att_send.at[d - 1], att_recv.at[d - 1], t, hi)
        )
    pending += att_copies
    loads[5].wait()
    wdn_t[...] = wdn[...].astype(F32).T.astype(BF16)
    for d in range(1, n):
        s = lax.rem(me - d + n, n)
        there = att.at[lax.rem(s, 2) * m + lax.div(s, 2)]
        pltpu.make_async_remote_copy(
            src_ref=there, dst_ref=there, send_sem=att_send.at[d - 1],
            recv_sem=att_recv.at[d - 1], device_id=(s, hi), device_id_type=MESH,
        ).wait_recv()

    def sum_heads(part, which):
        held = ar.at[which]
        held[hi] = part.astype(BF16)
        copies = []
        for d in range(1, heads_axis):
            copies.append(
                send(held.at[hi], held.at[hi], ar_send.at[which, d - 1],
                     ar_recv.at[which, d - 1], me, lax.rem(hi + d, heads_axis))
            )
        pending.extend(copies)
        for d in range(1, heads_axis):
            there = held.at[lax.rem(hi - d + heads_axis, heads_axis)]
            pltpu.make_async_remote_copy(
                src_ref=there, dst_ref=there, send_sem=ar_send.at[which, d - 1],
                recv_sem=ar_recv.at[which, d - 1],
                device_id=(me, lax.rem(hi - d + heads_axis, heads_axis)), device_id_type=MESH,
            ).wait_recv()
        whole = held[0].astype(F32)
        for h in range(1, heads_axis):
            whole = whole + held[h].astype(F32)
        return whole

    eye = lax.broadcasted_iota(jnp.int32, (total_rows, total_rows), 0) == lax.broadcasted_iota(
        jnp.int32, (total_rows, total_rows), 1
    )

    def inverse_rms(part, which):
        power = jnp.sum(part * part, axis=1, keepdims=True)
        flat = jnp.sum(jnp.where(eye, power, 0.0), axis=0, keepdims=True)
        pw_src[which] = jnp.broadcast_to(flat, (8, total_rows))
        copies = []
        for d in range(1, n):
            copies.append(
                send(pw_src.at[which], pw_dst.at[which, d - 1], pw_send.at[which, d - 1],
                     pw_recv.at[which, d - 1], lax.rem(me + d, n), hi)
            )
        pending.extend(copies)
        for d in range(1, n):
            copies[d - 1].wait_recv()
            flat = flat + pw_dst[which, d - 1, 0:1, :]
        scaled = lax.rsqrt(flat / model_width + EPS)
        return jnp.sum(jnp.where(eye, scaled, 0.0), axis=1, keepdims=True)

    small_loads[2].wait()
    attn = sum_heads(dot(att[...].reshape(total_rows, width), wout_t[...]), 0)
    attn = attn * inverse_rms(attn, 0) * ng[0:1, :]
    hm[...] = (hp[...].astype(F32) + attn).astype(BF16)

    units = wgu.shape[2]
    cu = units // CHUNKS
    loads[4].wait()
    gy_copies = []
    for c in range(CHUNKS):
        cols = pl.ds(c * cu, cu)
        gp[c, :, :, :, :cu] = dot(hm[...], wgu[0, :, cols]).astype(BF16).reshape(2, m, rows, cu)
        gp[c, :, :, :, cu:] = dot(hm[...], wgu[1, :, cols]).astype(BF16).reshape(2, m, rows, cu)
        gy_copies.append(
            send(gp.at[c, 1 - yi], gy.at[c], gy_send.at[c], gy_recv.at[c], ypart, hi)
        )
    pending += gy_copies
    gz_copies = {}
    ay_copies = {}
    az_copies = {}
    state = {"down": None}

    def pair_sum(c):
        gy_copies[c].wait_recv()
        gs[c] = (gp[c, yi].astype(F32) + gy[c].astype(F32)).astype(BF16)
        for d in range(1, m):
            t = lax.rem(zi + d, m)
            gz_copies[c, d] = send(gs.at[c, t], gz.at[c, d - 1], gz_send.at[c, d - 1],
                                   gz_recv.at[c, d - 1], t * 2 + yi, hi)
            pending.append(gz_copies[c, d])

    def activate(c):
        full = gs[c, zi].astype(F32)
        for d in range(1, m):
            gz_copies[c, d].wait_recv()
            full = full + gz[c, d - 1].astype(F32)
        gate = full[:, :cu]
        act[c, slot] = (gate / (1.0 + jnp.exp(-gate)) * full[:, cu:]).astype(BF16)
        for d in range(1, m):
            t = lax.rem(zi + d, m)
            az_copies[c, d] = send(act.at[c, slot], act.at[c, slot], az_send.at[c, d - 1],
                                   az_recv.at[c, d - 1], t * 2 + yi, hi)
            pending.append(az_copies[c, d])

    def forward(c):
        for d in range(1, m):
            s = lax.rem(zi - d + m, m)
            there = act.at[c, yi * m + s]
            pltpu.make_async_remote_copy(
                src_ref=there, dst_ref=there, send_sem=az_send.at[c, d - 1],
                recv_sem=az_recv.at[c, d - 1], device_id=(s * 2 + yi, hi), device_id_type=MESH,
            ).wait_recv()
        mine = act.at[c, pl.ds(yi * m, m)]
        ay_copies[c] = send(mine, mine, ay_send.at[c], ay_recv.at[c], ypart, hi)
        pending.append(ay_copies[c])

    def project(c):
        other = act.at[c, pl.ds((1 - yi) * m, m)]
        pltpu.make_async_remote_copy(
            src_ref=other, dst_ref=other, send_sem=ay_send.at[c], recv_sem=ay_recv.at[c],
            device_id=(ypart, hi), device_id_type=MESH,
        ).wait_recv()
        part = dot(act[c].reshape(total_rows, cu), wdn_t[pl.ds(c * cu, cu), :])
        state["down"] = part if state["down"] is None else state["down"] + part

    stages = (pair_sum, activate, forward, project)
    for step in range(CHUNKS + len(stages) - 1):
        for k, stage in enumerate(stages):
            if 0 <= step - k < CHUNKS:
                stage(step - k)
    ffn = sum_heads(state["down"], 1)
    ffn = ffn * inverse_rms(ffn, 1) * ng[1:2, :]
    result = (hm[...].astype(F32) + ffn).astype(BF16)
    for y in range(2):
        for z in range(m):
            p = (y * m + z) * rows
            out[pl.ds((z * 2 + y) * rows, rows), :] = result[p : p + rows]
    for copy in pending:
        copy.wait_send()


def body(
    n, heads_axis,
    hidden_in, lengths, w_qkv, qk_gain, cache_keys, cache_values,
    w_out, norm_gain, w_gate_up, w_down,
):
    rows = lengths.shape[0]
    total_rows, feat = hidden_in.shape
    width = w_qkv.shape[2]
    heads = width // HEAD_DIM
    units = w_gate_up.shape[2]
    m = n // 2
    cu = units // CHUNKS
    half = HEAD_DIM // 2
    freqs = np.power(THETA, -(np.arange(half, dtype=np.float64) * 2.0 / HEAD_DIM))
    freqs = np.broadcast_to(np.concatenate([freqs, freqs]), (8, HEAD_DIM)).astype(np.float32)
    dma = pltpu.SemaphoreType.DMA
    vmem = pltpu.VMEM
    scratch = [
        vmem(w_qkv.shape, BF16), vmem(cache_keys.shape, BF16), vmem(cache_values.shape, BF16),
        vmem(w_out.shape, BF16), vmem(w_gate_up.shape, BF16), vmem(w_down.shape, BF16),
        vmem(w_out.shape[::-1], BF16), vmem(w_down.shape[::-1], BF16), dma((6,)),
        vmem(hidden_in.shape, BF16), vmem(qk_gain.shape, F32), vmem(norm_gain.shape, F32),
        vmem((8, HEAD_DIM), F32), dma((4,)),
        vmem((total_rows, feat), BF16),
        vmem((n, rows, width), BF16), vmem((n - 1, rows, width), BF16),
        vmem((n, rows, width), BF16), vmem((n - 1, rows, width), BF16),
        vmem((n, rows, width), BF16), vmem((n - 1, rows, width), BF16),
        dma((3, n - 1)), dma((3, n - 1)),
        vmem((2, rows, HEAD_DIM), F32), vmem((2, heads_axis - 1, rows, HEAD_DIM), F32),
        dma((2, heads_axis - 1)), dma((2, heads_axis - 1)),
        vmem((heads * rows, cache_keys.shape[0]), F32),
        vmem((n, rows, width), BF16), dma((n - 1,)), dma((n - 1,)),
        vmem((2, heads_axis, total_rows, feat), BF16),
        dma((2, heads_axis - 1)), dma((2, heads_axis - 1)),
        vmem((2, 8, total_rows), F32), vmem((2, n - 1, 8, total_rows), F32),
        dma((2, n - 1)), dma((2, n - 1)),
        vmem((total_rows, feat), BF16),
        vmem((CHUNKS, 2, m, rows, 2 * cu), BF16), vmem((CHUNKS, m, rows, 2 * cu), BF16),
        vmem((CHUNKS, m, rows, 2 * cu), BF16), vmem((CHUNKS, m - 1, rows, 2 * cu), BF16),
        dma((CHUNKS,)), dma((CHUNKS,)), dma((CHUNKS, m - 1)), dma((CHUNKS, m - 1)),
        vmem((CHUNKS, n, rows, cu), BF16),
        dma((CHUNKS, m - 1)), dma((CHUNKS, m - 1)), dma((CHUNKS,)), dma((CHUNKS,)),
    ]
    in_vmem = pl.BlockSpec(memory_space=pltpu.VMEM)
    anywhere = pl.BlockSpec(memory_space=pl.ANY)
    outs = pl.pallas_call(
        functools.partial(kernel, n, heads_axis, feat * n),
        out_shape=(
            jax.ShapeDtypeStruct((total_rows, feat), BF16),
            jax.ShapeDtypeStruct((rows, width), BF16),
            jax.ShapeDtypeStruct((rows, width), BF16),
        ),
        in_specs=[pl.BlockSpec(memory_space=pltpu.SMEM)] + [anywhere] * 10,
        out_specs=(in_vmem,) * 3,
        scratch_shapes=scratch,
        compiler_params=pltpu.CompilerParams(
            collective_id=0, has_side_effects=True, vmem_limit_bytes=56 * 1024 * 1024
        ),
    )(
        lengths, hidden_in, qk_gain, norm_gain, jnp.asarray(freqs),
        w_qkv, cache_keys, cache_values, w_out, w_gate_up, w_down,
    )
    return pl.pallas_call(
        place_outputs,
        out_shape=tuple(jax.ShapeDtypeStruct(a.shape, a.dtype) for a in outs),
        in_specs=[in_vmem] * 3,
        out_specs=(in_vmem,) * 3,
    )(*outs)


def solution(mesh):
    return jax.shard_map(
        functools.partial(body, mesh.shape["req"], mesh.shape["head"]),
        mesh=mesh,
        in_specs=(
            P(None, "req"),
            P("req"),
            P(None, "req", "head"),
            P(None, "head"),
            P("req", "head"),
            P("req", "head"),
            P("req", "head"),
            P(None, "req"),
            P(None, "req", "head"),
            P("req", "head"),
        ),
        out_specs=(P(None, "req"), P("req", "head"), P("req", "head")),
        check_vma=False,
    )
```

```python
import functools

import jax
import jax.numpy as jnp
import numpy as np
from jax import lax
from jax.experimental import pallas as pl
from jax.experimental.pallas import tpu as pltpu
from jax.sharding import PartitionSpec as P

HEAD_DIM = 128
EPS = 1e-06
THETA = 500000.0
MESH = pl.DeviceIdType.MESH
F32 = jnp.float32
BF16 = jnp.bfloat16
CHUNKS = 4
KEY_BLOCK = 512


def dot(left, right):
    return lax.dot_general(left, right, (((1,), (0,)), ((), ())), preferred_element_type=F32)


def dot_last(left, right):
    return lax.dot_general(left, right, (((1,), (1,)), ((), ())), preferred_element_type=F32)


def place_outputs(a, b, c, out_a, out_b, out_c):
    out_a[...] = a[...]
    out_b[...] = b[...]
    out_c[...] = c[...]


def kernel(
    n, heads_axis, model_width,
    lens, hid_h, qkg_h, ng_h, freq_h, wqkv_h, ck_h, cv_h, wout_h, wgu_h, wdn_h,
    out, nk, nv,
    wqkv, ck, cv, wout, wgu, wdn, load_sem,
    hid, qkg, ng, freq, small_sem,
    hp, pq, zq, pkv, zkv, rs_send, rs_recv,
    sqs, sqr, sq_send, sq_recv,
    scores, numer, att, att_send, att_recv,
    ar, ar_send, ar_recv,
    pw_src, pw_dst, pw_send, pw_recv,
    hm, gp, gy, gs, gz, gy_send, gy_recv, gz_send, gz_recv,
    act, az_send, az_recv, ay_send, ay_recv,
):
    me = lax.axis_index("req")
    hi = lax.axis_index("head")
    m = n // 2
    zi = lax.div(me, 2)
    yi = lax.rem(me, 2)
    rows = lens.shape[0]
    width = qkg.shape[1]
    heads = width // HEAD_DIM
    total_rows = n * rows
    slot = yi * m + zi
    ypart = zi * 2 + (1 - yi)

    def loader(index, src, dst):
        return pltpu.make_async_copy(src, dst, load_sem.at[index])

    loads = [
        loader(0, wqkv_h, wqkv), loader(1, ck_h, ck), loader(2, cv_h, cv),
        loader(3, wout_h, wout), loader(4, wgu_h, wgu), loader(5, wdn_h, wdn),
    ]
    small_loads = [
        pltpu.make_async_copy(src, dst, small_sem.at[i])
        for i, (src, dst) in enumerate(((hid_h, hid), (qkg_h, qkg), (ng_h, ng), (freq_h, freq)))
    ]
    small_loads[0].start()
    loads[0].start()
    for load in small_loads[1:]:
        load.start()

    barrier = pltpu.get_barrier_semaphore()
    for d in range(1, n):
        pl.semaphore_signal(barrier, inc=1, device_id=(lax.rem(me + d, n), hi), device_id_type=MESH)
    for d in range(1, heads_axis):
        pl.semaphore_signal(
            barrier, inc=1, device_id=(me, lax.rem(hi + d, heads_axis)), device_id_type=MESH
        )

    def send(src, dst, ssem, rsem, req, head):
        copy = pltpu.make_async_remote_copy(
            src_ref=src, dst_ref=dst, send_sem=ssem, recv_sem=rsem,
            device_id=(req, head), device_id_type=MESH,
        )
        copy.start()
        return copy

    pending = []

    small_loads[0].wait()
    for y in range(2):
        for z in range(m):
            hp[pl.ds((y * m + z) * rows, rows), :] = hid[pl.ds((z * 2 + y) * rows, rows), :]
    loads[0].wait()
    for load in loads[1:]:
        load.start()
    x = hp[...]
    pq[...] = dot(x, wqkv[0]).astype(BF16).reshape(n, rows, width)
    pl.semaphore_wait(barrier, n - 1 + heads_axis - 1)

    def scatter(src, dst, which):
        copies = []
        for d in range(1, n):
            t = lax.rem(me + d, n)
            place = lax.rem(t, 2) * m + lax.div(t, 2)
            copies.append(
                send(src.at[place], dst.at[d - 1], rs_send.at[which, d - 1],
                     rs_recv.at[which, d - 1], t, hi)
            )
        pending.extend(copies)
        return copies

    def gathered(src, dst, copies):
        total = src[slot].astype(F32)
        for d in range(1, n):
            copies[d - 1].wait_recv()
            total = total + dst[d - 1].astype(F32)
        return total

    zq_copies = scatter(pq, zq, 0)
    pkv[:, :, :width] = dot(x, wqkv[1]).astype(BF16).reshape(n, rows, width)
    pkv[:, :, width:] = dot(x, wqkv[2]).astype(BF16).reshape(n, rows, width)
    zkv_copies = scatter(pkv, zkv, 1)

    row_id = lax.broadcasted_iota(jnp.int32, (rows, HEAD_DIM), 0)
    lane = lax.broadcasted_iota(jnp.int32, (rows, HEAD_DIM), 1)
    starts = jnp.zeros((rows, HEAD_DIM), jnp.int32)
    lengths = jnp.zeros((rows, HEAD_DIM), jnp.int32)
    at = jnp.int32(0)
    for r in range(rows):
        length = lens[r]
        starts = jnp.where(row_id == r, at, starts)
        lengths = jnp.where(row_id == r, length, lengths)
        at = at + length
    ends = starts + lengths
    small_loads[3].wait()
    angles = lengths.astype(F32) * freq[0:1, :]
    cosine = jnp.cos(angles)
    sine = jnp.sin(angles)
    sine = jnp.where(lane < HEAD_DIM // 2, -sine, sine)

    small_loads[1].wait()
    query = gathered(pq, zq, zq_copies)

    def share_power(values, which):
        power = jnp.sum(values * values, axis=1, keepdims=True)
        sqs[which] = jnp.broadcast_to(power, (rows, HEAD_DIM))
        copies = []
        for d in range(1, heads_axis):
            copies.append(
                send(sqs.at[which], sqr.at[which, d - 1], sq_send.at[which, d - 1],
                     sq_recv.at[which, d - 1], me, lax.rem(hi + d, heads_axis))
            )
        pending.extend(copies)
        return copies

    def inverse_root(copies, which):
        power = sqs[which]
        for d in range(1, heads_axis):
            copies[d - 1].wait_recv()
            power = power + sqr[which, d - 1]
        return lax.rsqrt(power[:, 0:1] / (width * heads_axis) + EPS)

    def rotate(values):
        parts = []
        for h in range(heads):
            part = values[:, h * HEAD_DIM : (h + 1) * HEAD_DIM]
            parts.append(part * cosine + pltpu.roll(part, HEAD_DIM // 2, 1) * sine)
        return jnp.concatenate(parts, axis=1)

    q_copies = share_power(query, 0)
    query_rot = rotate(query * qkg[0:1, :]).astype(BF16).astype(F32)

    scale = HEAD_DIM ** (-0.5)
    wide_lane = lax.broadcasted_iota(jnp.int32, (rows, width), 1)
    q_rows = []
    for h in range(heads):
        inside = (wide_lane >= h * HEAD_DIM) & (wide_lane < (h + 1) * HEAD_DIM)
        q_rows.append(jnp.where(inside, query_rot, 0.0))
    q_all = jnp.concatenate(q_rows, axis=0).astype(BF16)
    first = jnp.concatenate([starts[:, 0:1]] * heads, axis=0)
    last = jnp.concatenate([ends[:, 0:1]] * heads, axis=0)
    pool = ck.shape[0]
    loads[1].wait()
    q_scale = jnp.concatenate([inverse_root(q_copies, 0) * scale] * heads, axis=0)
    column = lax.broadcasted_iota(jnp.int32, (heads * rows, KEY_BLOCK), 1)
    blocks = pool // KEY_BLOCK

    def score_block(b, highest):
        start = pl.multiple_of(b * KEY_BLOCK, KEY_BLOCK)
        span = pl.ds(start, KEY_BLOCK)
        s = dot_last(q_all, ck[span, :]) * q_scale
        place = start + column
        s = jnp.where((place >= first) & (place < last), s, -1e30)
        scores[b] = s
        return jnp.maximum(highest, jnp.max(s, axis=1, keepdims=True))

    highest = lax.fori_loop(
        0, blocks, score_block, jnp.full((heads * rows, 1), -1e30, F32)
    )

    both = gathered(pkv, zkv, zkv_copies)
    key_new = both[:, :width]
    value_new = both[:, width:].astype(BF16)
    nv[...] = value_new
    k_copies = share_power(key_new, 1)

    loads[2].wait()
    numer[...] = jnp.zeros_like(numer)

    def value_block(b, total):
        span = pl.ds(pl.multiple_of(b * KEY_BLOCK, KEY_BLOCK), KEY_BLOCK)
        w = jnp.exp(scores[b] - highest).astype(BF16)
        numer[...] += dot(w, cv[span, :])
        return total + jnp.sum(w.astype(F32), axis=1, keepdims=True)

    denominator = lax.fori_loop(
        0, blocks, value_block, jnp.zeros((heads * rows, 1), F32)
    )
    numerator = numer[...]

    key_rot = rotate(key_new * inverse_root(k_copies, 1) * qkg[1:2, :]).astype(BF16)
    nk[...] = key_rot
    own = query_rot * key_rot.astype(F32)
    own = jnp.concatenate(
        [
            jnp.sum(own[:, h * HEAD_DIM : (h + 1) * HEAD_DIM], axis=1, keepdims=True)
            for h in range(heads)
        ],
        axis=0,
    ) * q_scale
    top = jnp.maximum(highest, own)
    factor = jnp.exp(highest - top)
    own_weight = jnp.exp(own - top).astype(BF16).astype(F32)
    denominator = denominator * factor + own_weight
    numerator = numerator * factor + own_weight * jnp.concatenate(
        [value_new.astype(F32)] * heads, axis=0
    )
    ratio = numerator / denominator
    attended = jnp.concatenate(
        [
            ratio[h * rows : (h + 1) * rows, h * HEAD_DIM : (h + 1) * HEAD_DIM]
            for h in range(heads)
        ],
        axis=1,
    ).astype(BF16)
    att[slot] = attended
    att_copies = []
    for d in range(1, n):
        t = lax.rem(me + d, n)
        att_copies.append(
            send(att.at[slot], att.at[slot], att_send.at[d - 1], att_recv.at[d - 1], t, hi)
        )
    pending += att_copies
    for d in range(1, n):
        s = lax.rem(me - d + n, n)
        there = att.at[lax.rem(s, 2) * m + lax.div(s, 2)]
        pltpu.make_async_remote_copy(
            src_ref=there, dst_ref=there, send_sem=att_send.at[d - 1],
            recv_sem=att_recv.at[d - 1], device_id=(s, hi), device_id_type=MESH,
        ).wait_recv()

    def sum_heads(part, which):
        held = ar.at[which]
        held[hi] = part.astype(BF16)
        copies = []
        for d in range(1, heads_axis):
            copies.append(
                send(held.at[hi], held.at[hi], ar_send.at[which, d - 1],
                     ar_recv.at[which, d - 1], me, lax.rem(hi + d, heads_axis))
            )
        pending.extend(copies)
        for d in range(1, heads_axis):
            there = held.at[lax.rem(hi - d + heads_axis, heads_axis)]
            pltpu.make_async_remote_copy(
                src_ref=there, dst_ref=there, send_sem=ar_send.at[which, d - 1],
                recv_sem=ar_recv.at[which, d - 1],
                device_id=(me, lax.rem(hi - d + heads_axis, heads_axis)), device_id_type=MESH,
            ).wait_recv()
        whole = held[0].astype(F32)
        for h in range(1, heads_axis):
            whole = whole + held[h].astype(F32)
        return whole

    eye = lax.broadcasted_iota(jnp.int32, (total_rows, total_rows), 0) == lax.broadcasted_iota(
        jnp.int32, (total_rows, total_rows), 1
    )

    def inverse_rms(part, which):
        power = jnp.sum(part * part, axis=1, keepdims=True)
        flat = jnp.sum(jnp.where(eye, power, 0.0), axis=0, keepdims=True)
        pw_src[which] = jnp.broadcast_to(flat, (8, total_rows))
        copies = []
        for d in range(1, n):
            copies.append(
                send(pw_src.at[which], pw_dst.at[which, d - 1], pw_send.at[which, d - 1],
                     pw_recv.at[which, d - 1], lax.rem(me + d, n), hi)
            )
        pending.extend(copies)
        for d in range(1, n):
            copies[d - 1].wait_recv()
            flat = flat + pw_dst[which, d - 1, 0:1, :]
        scaled = lax.rsqrt(flat / model_width + EPS)
        return jnp.sum(jnp.where(eye, scaled, 0.0), axis=1, keepdims=True)

    small_loads[2].wait()
    loads[3].wait()
    attn = sum_heads(dot_last(att[...].reshape(total_rows, width), wout[...]), 0)
    attn = attn * inverse_rms(attn, 0) * ng[0:1, :]
    hm[...] = (hp[...].astype(F32) + attn).astype(BF16)

    units = wgu.shape[2]
    cu = units // CHUNKS
    loads[4].wait()
    gy_copies = []
    for c in range(CHUNKS):
        cols = pl.ds(c * cu, cu)
        gp[c, :, :, :, :cu] = dot(hm[...], wgu[0, :, cols]).astype(BF16).reshape(2, m, rows, cu)
        gp[c, :, :, :, cu:] = dot(hm[...], wgu[1, :, cols]).astype(BF16).reshape(2, m, rows, cu)
        gy_copies.append(
            send(gp.at[c, 1 - yi], gy.at[c], gy_send.at[c], gy_recv.at[c], ypart, hi)
        )
    pending += gy_copies
    gz_copies = {}
    ay_copies = {}
    az_copies = {}
    state = {"down": None}

    def pair_sum(c):
        gy_copies[c].wait_recv()
        gs[c] = (gp[c, yi].astype(F32) + gy[c].astype(F32)).astype(BF16)
        for d in range(1, m):
            t = lax.rem(zi + d, m)
            gz_copies[c, d] = send(gs.at[c, t], gz.at[c, d - 1], gz_send.at[c, d - 1],
                                   gz_recv.at[c, d - 1], t * 2 + yi, hi)
            pending.append(gz_copies[c, d])

    def activate(c):
        full = gs[c, zi].astype(F32)
        for d in range(1, m):
            gz_copies[c, d].wait_recv()
            full = full + gz[c, d - 1].astype(F32)
        gate = full[:, :cu]
        act[c, slot] = (gate / (1.0 + jnp.exp(-gate)) * full[:, cu:]).astype(BF16)
        for d in range(1, m):
            t = lax.rem(zi + d, m)
            az_copies[c, d] = send(act.at[c, slot], act.at[c, slot], az_send.at[c, d - 1],
                                   az_recv.at[c, d - 1], t * 2 + yi, hi)
            pending.append(az_copies[c, d])

    def forward(c):
        for d in range(1, m):
            s = lax.rem(zi - d + m, m)
            there = act.at[c, yi * m + s]
            pltpu.make_async_remote_copy(
                src_ref=there, dst_ref=there, send_sem=az_send.at[c, d - 1],
                recv_sem=az_recv.at[c, d - 1], device_id=(s * 2 + yi, hi), device_id_type=MESH,
            ).wait_recv()
        mine = act.at[c, pl.ds(yi * m, m)]
        ay_copies[c] = send(mine, mine, ay_send.at[c], ay_recv.at[c], ypart, hi)
        pending.append(ay_copies[c])

    def project(c):
        other = act.at[c, pl.ds((1 - yi) * m, m)]
        pltpu.make_async_remote_copy(
            src_ref=other, dst_ref=other, send_sem=ay_send.at[c], recv_sem=ay_recv.at[c],
            device_id=(ypart, hi), device_id_type=MESH,
        ).wait_recv()
        if c == 0:
            loads[5].wait()
        part = dot_last(act[c].reshape(total_rows, cu), wdn[:, pl.ds(c * cu, cu)])
        state["down"] = part if state["down"] is None else state["down"] + part

    stages = (pair_sum, activate, forward, project)
    for step in range(CHUNKS + len(stages) - 1):
        for k, stage in enumerate(stages):
            if 0 <= step - k < CHUNKS:
                stage(step - k)
    ffn = sum_heads(state["down"], 1)
    ffn = ffn * inverse_rms(ffn, 1) * ng[1:2, :]
    result = (hm[...].astype(F32) + ffn).astype(BF16)
    for y in range(2):
        for z in range(m):
            p = (y * m + z) * rows
            out[pl.ds((z * 2 + y) * rows, rows), :] = result[p : p + rows]
    for copy in pending:
        copy.wait_send()


def body(
    n, heads_axis,
    hidden_in, lengths, w_qkv, qk_gain, cache_keys, cache_values,
    w_out, norm_gain, w_gate_up, w_down,
):
    rows = lengths.shape[0]
    total_rows, feat = hidden_in.shape
    width = w_qkv.shape[2]
    heads = width // HEAD_DIM
    units = w_gate_up.shape[2]
    m = n // 2
    cu = units // CHUNKS
    half = HEAD_DIM // 2
    freqs = np.power(THETA, -(np.arange(half, dtype=np.float64) * 2.0 / HEAD_DIM))
    freqs = np.broadcast_to(np.concatenate([freqs, freqs]), (8, HEAD_DIM)).astype(np.float32)
    dma = pltpu.SemaphoreType.DMA
    vmem = pltpu.VMEM
    scratch = [
        vmem(w_qkv.shape, BF16), vmem(cache_keys.shape, BF16), vmem(cache_values.shape, BF16),
        vmem(w_out.shape, BF16), vmem(w_gate_up.shape, BF16), vmem(w_down.shape, BF16),
        dma((6,)),
        vmem(hidden_in.shape, BF16), vmem(qk_gain.shape, F32), vmem(norm_gain.shape, F32),
        vmem((8, HEAD_DIM), F32), dma((4,)),
        vmem((total_rows, feat), BF16),
        vmem((n, rows, width), BF16), vmem((n - 1, rows, width), BF16),
        vmem((n, rows, 2 * width), BF16), vmem((n - 1, rows, 2 * width), BF16),
        dma((2, n - 1)), dma((2, n - 1)),
        vmem((2, rows, HEAD_DIM), F32), vmem((2, heads_axis - 1, rows, HEAD_DIM), F32),
        dma((2, heads_axis - 1)), dma((2, heads_axis - 1)),
        vmem((cache_keys.shape[0] // KEY_BLOCK, heads * rows, KEY_BLOCK), F32),
        vmem((heads * rows, width), F32),
        vmem((n, rows, width), BF16), dma((n - 1,)), dma((n - 1,)),
        vmem((2, heads_axis, total_rows, feat), BF16),
        dma((2, heads_axis - 1)), dma((2, heads_axis - 1)),
        vmem((2, 8, total_rows), F32), vmem((2, n - 1, 8, total_rows), F32),
        dma((2, n - 1)), dma((2, n - 1)),
        vmem((total_rows, feat), BF16),
        vmem((CHUNKS, 2, m, rows, 2 * cu), BF16), vmem((CHUNKS, m, rows, 2 * cu), BF16),
        vmem((CHUNKS, m, rows, 2 * cu), BF16), vmem((CHUNKS, m - 1, rows, 2 * cu), BF16),
        dma((CHUNKS,)), dma((CHUNKS,)), dma((CHUNKS, m - 1)), dma((CHUNKS, m - 1)),
        vmem((CHUNKS, n, rows, cu), BF16),
        dma((CHUNKS, m - 1)), dma((CHUNKS, m - 1)), dma((CHUNKS,)), dma((CHUNKS,)),
    ]
    in_vmem = pl.BlockSpec(memory_space=pltpu.VMEM)
    anywhere = pl.BlockSpec(memory_space=pl.ANY)
    outs = pl.pallas_call(
        functools.partial(kernel, n, heads_axis, feat * n),
        out_shape=(
            jax.ShapeDtypeStruct((total_rows, feat), BF16),
            jax.ShapeDtypeStruct((rows, width), BF16),
            jax.ShapeDtypeStruct((rows, width), BF16),
        ),
        in_specs=[pl.BlockSpec(memory_space=pltpu.SMEM)] + [anywhere] * 10,
        out_specs=(in_vmem,) * 3,
        scratch_shapes=scratch,
        compiler_params=pltpu.CompilerParams(
            collective_id=0, has_side_effects=True, vmem_limit_bytes=56 * 1024 * 1024
        ),
    )(
        lengths, hidden_in, qk_gain, norm_gain, jnp.asarray(freqs),
        w_qkv, cache_keys, cache_values, w_out, w_gate_up, w_down,
    )
    return pl.pallas_call(
        place_outputs,
        out_shape=tuple(jax.ShapeDtypeStruct(a.shape, a.dtype) for a in outs),
        in_specs=[in_vmem] * 3,
        out_specs=(in_vmem,) * 3,
    )(*outs)


def solution(mesh):
    return jax.shard_map(
        functools.partial(body, mesh.shape["req"], mesh.shape["head"]),
        mesh=mesh,
        in_specs=(
            P(None, "req"),
            P("req"),
            P(None, "req", "head"),
            P(None, "head"),
            P("req", "head"),
            P("req", "head"),
            P("req", "head"),
            P(None, "req"),
            P(None, "req", "head"),
            P("req", "head"),
        ),
        out_specs=(P(None, "req"), P("req", "head"), P("req", "head")),
        check_vma=False,
    )
```

```python
import functools

import jax
import jax.numpy as jnp
import numpy as np
from jax import lax
from jax.experimental import pallas as pl
from jax.experimental.pallas import tpu as pltpu
from jax.sharding import PartitionSpec as P

HEAD_DIM = 128
EPS = 1e-06
THETA = 500000.0
MESH = pl.DeviceIdType.MESH
F32 = jnp.float32
BF16 = jnp.bfloat16
CHUNKS = 4
IN_FLIGHT = 2
KEY_BLOCK = 512


def dot(left, right):
    return lax.dot_general(left, right, (((1,), (0,)), ((), ())), preferred_element_type=F32)


def place_outputs(a, b, c, out_a, out_b, out_c):
    out_a[...] = a[...]
    out_b[...] = b[...]
    out_c[...] = c[...]


def kernel(
    n, heads_axis, model_width,
    lens, hid_h, qkg_h, ng_h, freq_h, wqkv_h, ck_h, cv_h, wout_h, wgu_h, wdn_h,
    out, nk, nv,
    wqkv, ck, cv, wout, wgu, wdn, wout_t, wdn_t, load_sem,
    hid, qkg, ng, freq, small_sem,
    hp, pq, zq, pkv, zkv, rs_send, rs_recv,
    sqs, sqr, sq_send, sq_recv,
    scores, att, att_send, att_recv,
    ar, ar_send, ar_recv,
    pw_src, pw_dst, pw_send, pw_recv,
    hm, gp, gy, gs, gz, gy_send, gy_recv, gz_send, gz_recv,
    act, az_send, az_recv, ay_send, ay_recv,
):
    me = lax.axis_index("req")
    hi = lax.axis_index("head")
    m = n // 2
    zi = lax.div(me, 2)
    yi = lax.rem(me, 2)
    rows = lens.shape[0]
    width = qkg.shape[1]
    heads = width // HEAD_DIM
    total_rows = n * rows
    slot = yi * m + zi
    ypart = zi * 2 + (1 - yi)

    def loader(index, src, dst):
        return pltpu.make_async_copy(src, dst, load_sem.at[index])

    loads = [
        loader(0, wqkv_h, wqkv), loader(1, ck_h, ck), loader(2, cv_h, cv),
        loader(3, wout_h, wout), loader(4, wgu_h, wgu), loader(5, wdn_h, wdn),
    ]
    small_loads = [
        pltpu.make_async_copy(src, dst, small_sem.at[i])
        for i, (src, dst) in enumerate(((hid_h, hid), (qkg_h, qkg), (ng_h, ng), (freq_h, freq)))
    ]
    small_loads[0].start()
    loads[0].start()
    for load in small_loads[1:]:
        load.start()

    barrier = pltpu.get_barrier_semaphore()
    for d in range(1, n):
        pl.semaphore_signal(barrier, inc=1, device_id=(lax.rem(me + d, n), hi), device_id_type=MESH)
    for d in range(1, heads_axis):
        pl.semaphore_signal(
            barrier, inc=1, device_id=(me, lax.rem(hi + d, heads_axis)), device_id_type=MESH
        )

    def send(src, dst, ssem, rsem, req, head):
        copy = pltpu.make_async_remote_copy(
            src_ref=src, dst_ref=dst, send_sem=ssem, recv_sem=rsem,
            device_id=(req, head), device_id_type=MESH,
        )
        copy.start()
        return copy

    pending = []

    small_loads[0].wait()
    for y in range(2):
        for z in range(m):
            hp[pl.ds((y * m + z) * rows, rows), :] = hid[pl.ds((z * 2 + y) * rows, rows), :]
    loads[0].wait()
    for load in loads[1:]:
        load.start()
    x = hp[...]
    pq[...] = dot(x, wqkv[0]).astype(BF16).reshape(n, rows, width)
    pl.semaphore_wait(barrier, n - 1 + heads_axis - 1)

    def scatter(src, dst, which):
        copies = []
        for d in range(1, n):
            t = lax.rem(me + d, n)
            place = lax.rem(t, 2) * m + lax.div(t, 2)
            copies.append(
                send(src.at[place], dst.at[d - 1], rs_send.at[which, d - 1],
                     rs_recv.at[which, d - 1], t, hi)
            )
        pending.extend(copies)
        return copies

    def gathered(src, dst, copies):
        total = src[slot].astype(F32)
        for d in range(1, n):
            copies[d - 1].wait_recv()
            total = total + dst[d - 1].astype(F32)
        return total

    zq_copies = scatter(pq, zq, 0)
    pkv[:, :, :width] = dot(x, wqkv[1]).astype(BF16).reshape(n, rows, width)
    pkv[:, :, width:] = dot(x, wqkv[2]).astype(BF16).reshape(n, rows, width)

    row_id = lax.broadcasted_iota(jnp.int32, (rows, HEAD_DIM), 0)
    lane = lax.broadcasted_iota(jnp.int32, (rows, HEAD_DIM), 1)
    starts = jnp.zeros((rows, HEAD_DIM), jnp.int32)
    lengths = jnp.zeros((rows, HEAD_DIM), jnp.int32)
    at = jnp.int32(0)
    for r in range(rows):
        length = lens[r]
        starts = jnp.where(row_id == r, at, starts)
        lengths = jnp.where(row_id == r, length, lengths)
        at = at + length
    ends = starts + lengths
    small_loads[3].wait()
    angles = lengths.astype(F32) * freq[0:1, :]
    cosine = jnp.cos(angles)
    sine = jnp.sin(angles)
    sine = jnp.where(lane < HEAD_DIM // 2, -sine, sine)

    loads[3].wait()
    wout_t[...] = wout[...].astype(F32).T.astype(BF16)
    small_loads[1].wait()
    query = gathered(pq, zq, zq_copies)

    def share_power(values, which):
        power = jnp.sum(values * values, axis=1, keepdims=True)
        sqs[which] = jnp.broadcast_to(power, (rows, HEAD_DIM))
        copies = []
        for d in range(1, heads_axis):
            copies.append(
                send(sqs.at[which], sqr.at[which, d - 1], sq_send.at[which, d - 1],
                     sq_recv.at[which, d - 1], me, lax.rem(hi + d, heads_axis))
            )
        pending.extend(copies)
        return copies

    def inverse_root(copies, which):
        power = sqs[which]
        for d in range(1, heads_axis):
            copies[d - 1].wait_recv()
            power = power + sqr[which, d - 1]
        return lax.rsqrt(power[:, 0:1] / (width * heads_axis) + EPS)

    def rotate(values):
        parts = []
        for h in range(heads):
            part = values[:, h * HEAD_DIM : (h + 1) * HEAD_DIM]
            parts.append(part * cosine + pltpu.roll(part, HEAD_DIM // 2, 1) * sine)
        return jnp.concatenate(parts, axis=1)

    q_copies = share_power(query, 0)
    zkv_copies = scatter(pkv, zkv, 1)
    query_rot = rotate(query * qkg[0:1, :]).astype(BF16).astype(F32)

    scale = HEAD_DIM ** (-0.5)
    wide_lane = lax.broadcasted_iota(jnp.int32, (rows, width), 1)
    q_rows = []
    for h in range(heads):
        inside = (wide_lane >= h * HEAD_DIM) & (wide_lane < (h + 1) * HEAD_DIM)
        q_rows.append(jnp.where(inside, query_rot, 0.0))
    q_cols = jnp.concatenate(q_rows, axis=0).T.astype(BF16)
    first = jnp.concatenate([starts[:, 0:1]] * heads, axis=0)
    last = jnp.concatenate([ends[:, 0:1]] * heads, axis=0)
    pool = ck.shape[0]
    loads[1].wait()
    q_scale = jnp.concatenate([inverse_root(q_copies, 0) * scale] * heads, axis=0)
    highest = jnp.full((heads * rows, KEY_BLOCK), -1e30, F32)
    column = lax.broadcasted_iota(jnp.int32, (heads * rows, KEY_BLOCK), 1)
    for b in range(pool // KEY_BLOCK):
        span = pl.ds(b * KEY_BLOCK, KEY_BLOCK)
        s = dot(ck[span, :], q_cols).T * q_scale
        place = b * KEY_BLOCK + column
        s = jnp.where((place >= first) & (place < last), s, -1e30)
        scores[:, span] = s
        highest = jnp.maximum(highest, s)
    highest = jnp.max(highest, axis=1, keepdims=True)

    both = gathered(pkv, zkv, zkv_copies)
    key_new = both[:, :width]
    value_new = both[:, width:].astype(BF16)
    nv[...] = value_new
    k_copies = share_power(key_new, 1)

    total = jnp.zeros((heads * rows, KEY_BLOCK), F32)
    numerator = jnp.zeros((heads * rows, width), F32)
    loads[2].wait()
    for b in range(pool // KEY_BLOCK):
        span = pl.ds(b * KEY_BLOCK, KEY_BLOCK)
        w = jnp.exp(scores[:, span] - highest).astype(BF16)
        total = total + w.astype(F32)
        numerator = numerator + dot(w, cv[span, :])
    denominator = jnp.sum(total, axis=1, keepdims=True)

    key_rot = rotate(key_new * inverse_root(k_copies, 1) * qkg[1:2, :]).astype(BF16)
    nk[...] = key_rot
    own = query_rot * key_rot.astype(F32)
    own = jnp.concatenate(
        [
            jnp.sum(own[:, h * HEAD_DIM : (h + 1) * HEAD_DIM], axis=1, keepdims=True)
            for h in range(heads)
        ],
        axis=0,
    ) * q_scale
    top = jnp.maximum(highest, own)
    factor = jnp.exp(highest - top)
    own_weight = jnp.exp(own - top).astype(BF16).astype(F32)
    denominator = denominator * factor + own_weight
    numerator = numerator * factor + own_weight * jnp.concatenate(
        [value_new.astype(F32)] * heads, axis=0
    )
    ratio = numerator / denominator
    attended = jnp.concatenate(
        [
            ratio[h * rows : (h + 1) * rows, h * HEAD_DIM : (h + 1) * HEAD_DIM]
            for h in range(heads)
        ],
        axis=1,
    ).astype(BF16)
    att[slot] = attended
    att_copies = []
    for d in range(1, n):
        t = lax.rem(me + d, n)
        att_copies.append(
            send(att.at[slot], att.at[slot], att_send.at[d - 1], att_recv.at[d - 1], t, hi)
        )
    pending += att_copies
    loads[5].wait()
    wdn_t[...] = wdn[...].astype(F32).T.astype(BF16)
    for d in range(1, n):
        s = lax.rem(me - d + n, n)
        there = att.at[lax.rem(s, 2) * m + lax.div(s, 2)]
        pltpu.make_async_remote_copy(
            src_ref=there, dst_ref=there, send_sem=att_send.at[d - 1],
            recv_sem=att_recv.at[d - 1], device_id=(s, hi), device_id_type=MESH,
        ).wait_recv()

    def sum_heads(part, which):
        held = ar.at[which]
        held[hi] = part.astype(BF16)
        copies = []
        for d in range(1, heads_axis):
            copies.append(
                send(held.at[hi], held.at[hi], ar_send.at[which, d - 1],
                     ar_recv.at[which, d - 1], me, lax.rem(hi + d, heads_axis))
            )
        pending.extend(copies)
        for d in range(1, heads_axis):
            there = held.at[lax.rem(hi - d + heads_axis, heads_axis)]
            pltpu.make_async_remote_copy(
                src_ref=there, dst_ref=there, send_sem=ar_send.at[which, d - 1],
                recv_sem=ar_recv.at[which, d - 1],
                device_id=(me, lax.rem(hi - d + heads_axis, heads_axis)), device_id_type=MESH,
            ).wait_recv()
        whole = held[0].astype(F32)
        for h in range(1, heads_axis):
            whole = whole + held[h].astype(F32)
        return whole

    eye = lax.broadcasted_iota(jnp.int32, (total_rows, total_rows), 0) == lax.broadcasted_iota(
        jnp.int32, (total_rows, total_rows), 1
    )

    def inverse_rms(part, which):
        power = jnp.sum(part * part, axis=1, keepdims=True)
        flat = jnp.sum(jnp.where(eye, power, 0.0), axis=0, keepdims=True)
        pw_src[which] = jnp.broadcast_to(flat, (8, total_rows))
        copies = []
        for d in range(1, n):
            copies.append(
                send(pw_src.at[which], pw_dst.at[which, d - 1], pw_send.at[which, d - 1],
                     pw_recv.at[which, d - 1], lax.rem(me + d, n), hi)
            )
        pending.extend(copies)
        for d in range(1, n):
            copies[d - 1].wait_recv()
            flat = flat + pw_dst[which, d - 1, 0:1, :]
        scaled = lax.rsqrt(flat / model_width + EPS)
        return jnp.sum(jnp.where(eye, scaled, 0.0), axis=1, keepdims=True)

    small_loads[2].wait()
    attn = sum_heads(dot(att[...].reshape(total_rows, width), wout_t[...]), 0)
    attn = attn * inverse_rms(attn, 0) * ng[0:1, :]
    hm[...] = (hp[...].astype(F32) + attn).astype(BF16)

    units = wgu.shape[2]
    cu = units // CHUNKS
    loads[4].wait()
    gy_copies = {}

    def launch(c):
        cols = pl.ds(c * cu, cu)
        gp[c, :, :, :, :cu] = dot(hm[...], wgu[0, :, cols]).astype(BF16).reshape(2, m, rows, cu)
        gp[c, :, :, :, cu:] = dot(hm[...], wgu[1, :, cols]).astype(BF16).reshape(2, m, rows, cu)
        gy_copies[c] = send(gp.at[c, 1 - yi], gy.at[c], gy_send.at[c], gy_recv.at[c], ypart, hi)
        pending.append(gy_copies[c])

    for c in range(IN_FLIGHT):
        launch(c)
    gz_copies = {}
    ay_copies = {}
    az_copies = {}
    state = {"down": None}

    def pair_sum(c):
        gy_copies[c].wait_recv()
        gs[c] = (gp[c, yi].astype(F32) + gy[c].astype(F32)).astype(BF16)
        for d in range(1, m):
            t = lax.rem(zi + d, m)
            gz_copies[c, d] = send(gs.at[c, t], gz.at[c, d - 1], gz_send.at[c, d - 1],
                                   gz_recv.at[c, d - 1], t * 2 + yi, hi)
            pending.append(gz_copies[c, d])
        if c + IN_FLIGHT < CHUNKS:
            launch(c + IN_FLIGHT)

    def activate(c):
        full = gs[c, zi].astype(F32)
        for d in range(1, m):
            gz_copies[c, d].wait_recv()
            full = full + gz[c, d - 1].astype(F32)
        gate = full[:, :cu]
        act[c, slot] = (gate / (1.0 + jnp.exp(-gate)) * full[:, cu:]).astype(BF16)
        for d in range(1, m):
            t = lax.rem(zi + d, m)
            az_copies[c, d] = send(act.at[c, slot], act.at[c, slot], az_send.at[c, d - 1],
                                   az_recv.at[c, d - 1], t * 2 + yi, hi)
            pending.append(az_copies[c, d])

    def forward(c):
        for d in range(1, m):
            s = lax.rem(zi - d + m, m)
            there = act.at[c, yi * m + s]
            pltpu.make_async_remote_copy(
                src_ref=there, dst_ref=there, send_sem=az_send.at[c, d - 1],
                recv_sem=az_recv.at[c, d - 1], device_id=(s * 2 + yi, hi), device_id_type=MESH,
            ).wait_recv()
        mine = act.at[c, pl.ds(yi * m, m)]
        ay_copies[c] = send(mine, mine, ay_send.at[c], ay_recv.at[c], ypart, hi)
        pending.append(ay_copies[c])

    def project(c):
        other = act.at[c, pl.ds((1 - yi) * m, m)]
        pltpu.make_async_remote_copy(
            src_ref=other, dst_ref=other, send_sem=ay_send.at[c], recv_sem=ay_recv.at[c],
            device_id=(ypart, hi), device_id_type=MESH,
        ).wait_recv()
        part = dot(act[c].reshape(total_rows, cu), wdn_t[pl.ds(c * cu, cu), :])
        state["down"] = part if state["down"] is None else state["down"] + part

    stages = (pair_sum, activate, forward, project)
    for step in range(CHUNKS + len(stages) - 1):
        for k, stage in enumerate(stages):
            if 0 <= step - k < CHUNKS:
                stage(step - k)
    ffn = sum_heads(state["down"], 1)
    ffn = ffn * inverse_rms(ffn, 1) * ng[1:2, :]
    result = (hm[...].astype(F32) + ffn).astype(BF16)
    for y in range(2):
        for z in range(m):
            p = (y * m + z) * rows
            out[pl.ds((z * 2 + y) * rows, rows), :] = result[p : p + rows]
    for copy in pending:
        copy.wait_send()


def body(
    n, heads_axis,
    hidden_in, lengths, w_qkv, qk_gain, cache_keys, cache_values,
    w_out, norm_gain, w_gate_up, w_down,
):
    rows = lengths.shape[0]
    total_rows, feat = hidden_in.shape
    width = w_qkv.shape[2]
    heads = width // HEAD_DIM
    units = w_gate_up.shape[2]
    m = n // 2
    cu = units // CHUNKS
    half = HEAD_DIM // 2
    freqs = np.power(THETA, -(np.arange(half, dtype=np.float64) * 2.0 / HEAD_DIM))
    freqs = np.broadcast_to(np.concatenate([freqs, freqs]), (8, HEAD_DIM)).astype(np.float32)
    dma = pltpu.SemaphoreType.DMA
    vmem = pltpu.VMEM
    scratch = [
        vmem(w_qkv.shape, BF16), vmem(cache_keys.shape, BF16), vmem(cache_values.shape, BF16),
        vmem(w_out.shape, BF16), vmem(w_gate_up.shape, BF16), vmem(w_down.shape, BF16),
        vmem(w_out.shape[::-1], BF16), vmem(w_down.shape[::-1], BF16), dma((6,)),
        vmem(hidden_in.shape, BF16), vmem(qk_gain.shape, F32), vmem(norm_gain.shape, F32),
        vmem((8, HEAD_DIM), F32), dma((4,)),
        vmem((total_rows, feat), BF16),
        vmem((n, rows, width), BF16), vmem((n - 1, rows, width), BF16),
        vmem((n, rows, 2 * width), BF16), vmem((n - 1, rows, 2 * width), BF16),
        dma((2, n - 1)), dma((2, n - 1)),
        vmem((2, rows, HEAD_DIM), F32), vmem((2, heads_axis - 1, rows, HEAD_DIM), F32),
        dma((2, heads_axis - 1)), dma((2, heads_axis - 1)),
        vmem((heads * rows, cache_keys.shape[0]), F32),
        vmem((n, rows, width), BF16), dma((n - 1,)), dma((n - 1,)),
        vmem((2, heads_axis, total_rows, feat), BF16),
        dma((2, heads_axis - 1)), dma((2, heads_axis - 1)),
        vmem((2, 8, total_rows), F32), vmem((2, n - 1, 8, total_rows), F32),
        dma((2, n - 1)), dma((2, n - 1)),
        vmem((total_rows, feat), BF16),
        vmem((CHUNKS, 2, m, rows, 2 * cu), BF16), vmem((CHUNKS, m, rows, 2 * cu), BF16),
        vmem((CHUNKS, m, rows, 2 * cu), BF16), vmem((CHUNKS, m - 1, rows, 2 * cu), BF16),
        dma((CHUNKS,)), dma((CHUNKS,)), dma((CHUNKS, m - 1)), dma((CHUNKS, m - 1)),
        vmem((CHUNKS, n, rows, cu), BF16),
        dma((CHUNKS, m - 1)), dma((CHUNKS, m - 1)), dma((CHUNKS,)), dma((CHUNKS,)),
    ]
    in_vmem = pl.BlockSpec(memory_space=pltpu.VMEM)
    anywhere = pl.BlockSpec(memory_space=pl.ANY)
    outs = pl.pallas_call(
        functools.partial(kernel, n, heads_axis, feat * n),
        out_shape=(
            jax.ShapeDtypeStruct((total_rows, feat), BF16),
            jax.ShapeDtypeStruct((rows, width), BF16),
            jax.ShapeDtypeStruct((rows, width), BF16),
        ),
        in_specs=[pl.BlockSpec(memory_space=pltpu.SMEM)] + [anywhere] * 10,
        out_specs=(in_vmem,) * 3,
        scratch_shapes=scratch,
        compiler_params=pltpu.CompilerParams(
            collective_id=0, has_side_effects=True, vmem_limit_bytes=56 * 1024 * 1024
        ),
    )(
        lengths, hidden_in, qk_gain, norm_gain, jnp.asarray(freqs),
        w_qkv, cache_keys, cache_values, w_out, w_gate_up, w_down,
    )
    return pl.pallas_call(
        place_outputs,
        out_shape=tuple(jax.ShapeDtypeStruct(a.shape, a.dtype) for a in outs),
        in_specs=[in_vmem] * 3,
        out_specs=(in_vmem,) * 3,
    )(*outs)


def solution(mesh):
    return jax.shard_map(
        functools.partial(body, mesh.shape["req"], mesh.shape["head"]),
        mesh=mesh,
        in_specs=(
            P(None, "req"),
            P("req"),
            P(None, "req", "head"),
            P(None, "head"),
            P("req", "head"),
            P("req", "head"),
            P("req", "head"),
            P(None, "req"),
            P(None, "req", "head"),
            P("req", "head"),
        ),
        out_specs=(P(None, "req"), P("req", "head"), P("req", "head")),
        check_vma=False,
    )
```

```python
import functools

import jax
import jax.numpy as jnp
import numpy as np
from jax import lax
from jax.experimental import pallas as pl
from jax.experimental.pallas import tpu as pltpu
from jax.sharding import PartitionSpec as P

HEAD_DIM = 128
EPS = 1e-06
THETA = 500000.0
MESH = pl.DeviceIdType.MESH
F32 = jnp.float32
BF16 = jnp.bfloat16
CHUNKS = 2
IN_FLIGHT = 1
KEY_BLOCK = 512


def dot(left, right):
    return lax.dot_general(left, right, (((1,), (0,)), ((), ())), preferred_element_type=F32)


def place_outputs(a, b, c, out_a, out_b, out_c):
    out_a[...] = a[...]
    out_b[...] = b[...]
    out_c[...] = c[...]


def kernel(
    n, heads_axis, model_width,
    lens, hid_h, qkg_h, ng_h, freq_h, wqkv_h, ck_h, cv_h, wout_h, wgu_h, wdn_h,
    out, nk, nv,
    wqkv, ck, cv, wout, wgu, wdn, wout_t, wdn_t, load_sem,
    hid, qkg, ng, freq, small_sem,
    hp, pq, zq, pkv, zkv, rs_send, rs_recv,
    sqs, sqr, sq_send, sq_recv,
    scores, att, att_send, att_recv,
    ar, ar_send, ar_recv,
    pw_src, pw_dst, pw_send, pw_recv,
    hm, gp, gy, gs, gz, gy_send, gy_recv, gz_send, gz_recv,
    act, az_send, az_recv, ay_send, ay_recv,
):
    me = lax.axis_index("req")
    hi = lax.axis_index("head")
    m = n // 2
    zi = lax.div(me, 2)
    yi = lax.rem(me, 2)
    rows = lens.shape[0]
    width = qkg.shape[1]
    heads = width // HEAD_DIM
    total_rows = n * rows
    slot = yi * m + zi
    ypart = zi * 2 + (1 - yi)

    def loader(index, src, dst):
        return pltpu.make_async_copy(src, dst, load_sem.at[index])

    loads = [
        loader(0, wqkv_h, wqkv), loader(1, ck_h, ck), loader(2, cv_h, cv),
        loader(3, wout_h, wout), loader(4, wgu_h, wgu), loader(5, wdn_h, wdn),
    ]
    small_loads = [
        pltpu.make_async_copy(src, dst, small_sem.at[i])
        for i, (src, dst) in enumerate(((hid_h, hid), (qkg_h, qkg), (ng_h, ng), (freq_h, freq)))
    ]
    small_loads[0].start()
    loads[0].start()
    for load in small_loads[1:]:
        load.start()

    barrier = pltpu.get_barrier_semaphore()
    for d in range(1, n):
        pl.semaphore_signal(barrier, inc=1, device_id=(lax.rem(me + d, n), hi), device_id_type=MESH)
    for d in range(1, heads_axis):
        pl.semaphore_signal(
            barrier, inc=1, device_id=(me, lax.rem(hi + d, heads_axis)), device_id_type=MESH
        )

    def send(src, dst, ssem, rsem, req, head):
        copy = pltpu.make_async_remote_copy(
            src_ref=src, dst_ref=dst, send_sem=ssem, recv_sem=rsem,
            device_id=(req, head), device_id_type=MESH,
        )
        copy.start()
        return copy

    pending = []

    small_loads[0].wait()
    for y in range(2):
        for z in range(m):
            hp[pl.ds((y * m + z) * rows, rows), :] = hid[pl.ds((z * 2 + y) * rows, rows), :]
    loads[0].wait()
    for load in loads[1:]:
        load.start()
    x = hp[...]
    pq[...] = dot(x, wqkv[0]).astype(BF16).reshape(n, rows, width)
    pl.semaphore_wait(barrier, n - 1 + heads_axis - 1)

    def scatter(src, dst, which):
        copies = []
        for d in range(1, n):
            t = lax.rem(me + d, n)
            place = lax.rem(t, 2) * m + lax.div(t, 2)
            copies.append(
                send(src.at[place], dst.at[d - 1], rs_send.at[which, d - 1],
                     rs_recv.at[which, d - 1], t, hi)
            )
        pending.extend(copies)
        return copies

    def gathered(src, dst, copies):
        total = src[slot].astype(F32)
        for d in range(1, n):
            copies[d - 1].wait_recv()
            total = total + dst[d - 1].astype(F32)
        return total

    zq_copies = scatter(pq, zq, 0)
    pkv[:, :, :width] = dot(x, wqkv[1]).astype(BF16).reshape(n, rows, width)
    pkv[:, :, width:] = dot(x, wqkv[2]).astype(BF16).reshape(n, rows, width)

    row_id = lax.broadcasted_iota(jnp.int32, (rows, HEAD_DIM), 0)
    lane = lax.broadcasted_iota(jnp.int32, (rows, HEAD_DIM), 1)
    starts = jnp.zeros((rows, HEAD_DIM), jnp.int32)
    lengths = jnp.zeros((rows, HEAD_DIM), jnp.int32)
    at = jnp.int32(0)
    for r in range(rows):
        length = lens[r]
        starts = jnp.where(row_id == r, at, starts)
        lengths = jnp.where(row_id == r, length, lengths)
        at = at + length
    ends = starts + lengths
    small_loads[3].wait()
    angles = lengths.astype(F32) * freq[0:1, :]
    cosine = jnp.cos(angles)
    sine = jnp.sin(angles)
    sine = jnp.where(lane < HEAD_DIM // 2, -sine, sine)

    loads[3].wait()
    wout_t[...] = wout[...].astype(F32).T.astype(BF16)
    small_loads[1].wait()
    query = gathered(pq, zq, zq_copies)

    def share_power(values, which):
        power = jnp.sum(values * values, axis=1, keepdims=True)
        sqs[which] = jnp.broadcast_to(power, (rows, HEAD_DIM))
        copies = []
        for d in range(1, heads_axis):
            copies.append(
                send(sqs.at[which], sqr.at[which, d - 1], sq_send.at[which, d - 1],
                     sq_recv.at[which, d - 1], me, lax.rem(hi + d, heads_axis))
            )
        pending.extend(copies)
        return copies

    def inverse_root(copies, which):
        power = sqs[which]
        for d in range(1, heads_axis):
            copies[d - 1].wait_recv()
            power = power + sqr[which, d - 1]
        return lax.rsqrt(power[:, 0:1] / (width * heads_axis) + EPS)

    def rotate(values):
        parts = []
        for h in range(heads):
            part = values[:, h * HEAD_DIM : (h + 1) * HEAD_DIM]
            parts.append(part * cosine + pltpu.roll(part, HEAD_DIM // 2, 1) * sine)
        return jnp.concatenate(parts, axis=1)

    q_copies = share_power(query, 0)
    zkv_copies = scatter(pkv, zkv, 1)
    query_rot = rotate(query * qkg[0:1, :]).astype(BF16).astype(F32)

    scale = HEAD_DIM ** (-0.5)
    wide_lane = lax.broadcasted_iota(jnp.int32, (rows, width), 1)
    q_rows = []
    for h in range(heads):
        inside = (wide_lane >= h * HEAD_DIM) & (wide_lane < (h + 1) * HEAD_DIM)
        q_rows.append(jnp.where(inside, query_rot, 0.0))
    q_cols = jnp.concatenate(q_rows, axis=0).T.astype(BF16)
    first = jnp.concatenate([starts[:, 0:1]] * heads, axis=0)
    last = jnp.concatenate([ends[:, 0:1]] * heads, axis=0)
    pool = ck.shape[0]
    loads[1].wait()
    q_scale = jnp.concatenate([inverse_root(q_copies, 0) * scale] * heads, axis=0)
    highest = jnp.full((heads * rows, KEY_BLOCK), -1e30, F32)
    column = lax.broadcasted_iota(jnp.int32, (heads * rows, KEY_BLOCK), 1)
    for b in range(pool // KEY_BLOCK):
        span = pl.ds(b * KEY_BLOCK, KEY_BLOCK)
        s = dot(ck[span, :], q_cols).T * q_scale
        place = b * KEY_BLOCK + column
        s = jnp.where((place >= first) & (place < last), s, -1e30)
        scores[:, span] = s
        highest = jnp.maximum(highest, s)
    highest = jnp.max(highest, axis=1, keepdims=True)

    both = gathered(pkv, zkv, zkv_copies)
    key_new = both[:, :width]
    value_new = both[:, width:].astype(BF16)
    nv[...] = value_new
    k_copies = share_power(key_new, 1)

    total = jnp.zeros((heads * rows, KEY_BLOCK), F32)
    numerator = jnp.zeros((heads * rows, width), F32)
    loads[2].wait()
    for b in range(pool // KEY_BLOCK):
        span = pl.ds(b * KEY_BLOCK, KEY_BLOCK)
        w = jnp.exp(scores[:, span] - highest).astype(BF16)
        total = total + w.astype(F32)
        numerator = numerator + dot(w, cv[span, :])
    denominator = jnp.sum(total, axis=1, keepdims=True)

    key_rot = rotate(key_new * inverse_root(k_copies, 1) * qkg[1:2, :]).astype(BF16)
    nk[...] = key_rot
    own = query_rot * key_rot.astype(F32)
    own = jnp.concatenate(
        [
            jnp.sum(own[:, h * HEAD_DIM : (h + 1) * HEAD_DIM], axis=1, keepdims=True)
            for h in range(heads)
        ],
        axis=0,
    ) * q_scale
    top = jnp.maximum(highest, own)
    factor = jnp.exp(highest - top)
    own_weight = jnp.exp(own - top).astype(BF16).astype(F32)
    denominator = denominator * factor + own_weight
    numerator = numerator * factor + own_weight * jnp.concatenate(
        [value_new.astype(F32)] * heads, axis=0
    )
    ratio = numerator / denominator
    attended = jnp.concatenate(
        [
            ratio[h * rows : (h + 1) * rows, h * HEAD_DIM : (h + 1) * HEAD_DIM]
            for h in range(heads)
        ],
        axis=1,
    ).astype(BF16)
    att[slot] = attended
    att_copies = []
    for d in range(1, n):
        t = lax.rem(me + d, n)
        att_copies.append(
            send(att.at[slot], att.at[slot], att_send.at[d - 1], att_recv.at[d - 1], t, hi)
        )
    pending += att_copies
    loads[5].wait()
    wdn_t[...] = wdn[...].astype(F32).T.astype(BF16)
    for d in range(1, n):
        s = lax.rem(me - d + n, n)
        there = att.at[lax.rem(s, 2) * m + lax.div(s, 2)]
        pltpu.make_async_remote_copy(
            src_ref=there, dst_ref=there, send_sem=att_send.at[d - 1],
            recv_sem=att_recv.at[d - 1], device_id=(s, hi), device_id_type=MESH,
        ).wait_recv()

    def sum_heads(part, which):
        held = ar.at[which]
        held[hi] = part.astype(BF16)
        copies = []
        for d in range(1, heads_axis):
            copies.append(
                send(held.at[hi], held.at[hi], ar_send.at[which, d - 1],
                     ar_recv.at[which, d - 1], me, lax.rem(hi + d, heads_axis))
            )
        pending.extend(copies)
        for d in range(1, heads_axis):
            there = held.at[lax.rem(hi - d + heads_axis, heads_axis)]
            pltpu.make_async_remote_copy(
                src_ref=there, dst_ref=there, send_sem=ar_send.at[which, d - 1],
                recv_sem=ar_recv.at[which, d - 1],
                device_id=(me, lax.rem(hi - d + heads_axis, heads_axis)), device_id_type=MESH,
            ).wait_recv()
        whole = held[0].astype(F32)
        for h in range(1, heads_axis):
            whole = whole + held[h].astype(F32)
        return whole

    eye = lax.broadcasted_iota(jnp.int32, (total_rows, total_rows), 0) == lax.broadcasted_iota(
        jnp.int32, (total_rows, total_rows), 1
    )

    def inverse_rms(part, which):
        power = jnp.sum(part * part, axis=1, keepdims=True)
        flat = jnp.sum(jnp.where(eye, power, 0.0), axis=0, keepdims=True)
        pw_src[which] = jnp.broadcast_to(flat, (8, total_rows))
        copies = []
        for d in range(1, n):
            copies.append(
                send(pw_src.at[which], pw_dst.at[which, d - 1], pw_send.at[which, d - 1],
                     pw_recv.at[which, d - 1], lax.rem(me + d, n), hi)
            )
        pending.extend(copies)
        for d in range(1, n):
            copies[d - 1].wait_recv()
            flat = flat + pw_dst[which, d - 1, 0:1, :]
        scaled = lax.rsqrt(flat / model_width + EPS)
        return jnp.sum(jnp.where(eye, scaled, 0.0), axis=1, keepdims=True)

    small_loads[2].wait()
    attn = sum_heads(dot(att[...].reshape(total_rows, width), wout_t[...]), 0)
    attn = attn * inverse_rms(attn, 0) * ng[0:1, :]
    hm[...] = (hp[...].astype(F32) + attn).astype(BF16)

    units = wgu.shape[2]
    cu = units // CHUNKS
    loads[4].wait()
    gy_copies = {}

    def launch(c):
        cols = pl.ds(c * cu, cu)
        gp[c, :, :, :, :cu] = dot(hm[...], wgu[0, :, cols]).astype(BF16).reshape(2, m, rows, cu)
        gp[c, :, :, :, cu:] = dot(hm[...], wgu[1, :, cols]).astype(BF16).reshape(2, m, rows, cu)
        gy_copies[c] = send(gp.at[c, 1 - yi], gy.at[c], gy_send.at[c], gy_recv.at[c], ypart, hi)
        pending.append(gy_copies[c])

    for c in range(IN_FLIGHT):
        launch(c)
    gz_copies = {}
    ay_copies = {}
    az_copies = {}
    state = {"down": None}

    def pair_sum(c):
        gy_copies[c].wait_recv()
        gs[c] = (gp[c, yi].astype(F32) + gy[c].astype(F32)).astype(BF16)
        for d in range(1, m):
            t = lax.rem(zi + d, m)
            gz_copies[c, d] = send(gs.at[c, t], gz.at[c, d - 1], gz_send.at[c, d - 1],
                                   gz_recv.at[c, d - 1], t * 2 + yi, hi)
            pending.append(gz_copies[c, d])
        if c + IN_FLIGHT < CHUNKS:
            launch(c + IN_FLIGHT)

    def activate(c):
        full = gs[c, zi].astype(F32)
        for d in range(1, m):
            gz_copies[c, d].wait_recv()
            full = full + gz[c, d - 1].astype(F32)
        gate = full[:, :cu]
        act[c, slot] = (gate / (1.0 + jnp.exp(-gate)) * full[:, cu:]).astype(BF16)
        for d in range(1, m):
            t = lax.rem(zi + d, m)
            az_copies[c, d] = send(act.at[c, slot], act.at[c, slot], az_send.at[c, d - 1],
                                   az_recv.at[c, d - 1], t * 2 + yi, hi)
            pending.append(az_copies[c, d])

    def forward(c):
        for d in range(1, m):
            s = lax.rem(zi - d + m, m)
            there = act.at[c, yi * m + s]
            pltpu.make_async_remote_copy(
                src_ref=there, dst_ref=there, send_sem=az_send.at[c, d - 1],
                recv_sem=az_recv.at[c, d - 1], device_id=(s * 2 + yi, hi), device_id_type=MESH,
            ).wait_recv()
        mine = act.at[c, pl.ds(yi * m, m)]
        ay_copies[c] = send(mine, mine, ay_send.at[c], ay_recv.at[c], ypart, hi)
        pending.append(ay_copies[c])

    def project(c):
        other = act.at[c, pl.ds((1 - yi) * m, m)]
        pltpu.make_async_remote_copy(
            src_ref=other, dst_ref=other, send_sem=ay_send.at[c], recv_sem=ay_recv.at[c],
            device_id=(ypart, hi), device_id_type=MESH,
        ).wait_recv()
        part = dot(act[c].reshape(total_rows, cu), wdn_t[pl.ds(c * cu, cu), :])
        state["down"] = part if state["down"] is None else state["down"] + part

    stages = (pair_sum, activate, forward, project)
    for step in range(CHUNKS + len(stages) - 1):
        for k, stage in enumerate(stages):
            if 0 <= step - k < CHUNKS:
                stage(step - k)
    ffn = sum_heads(state["down"], 1)
    ffn = ffn * inverse_rms(ffn, 1) * ng[1:2, :]
    result = (hm[...].astype(F32) + ffn).astype(BF16)
    for y in range(2):
        for z in range(m):
            p = (y * m + z) * rows
            out[pl.ds((z * 2 + y) * rows, rows), :] = result[p : p + rows]
    for copy in pending:
        copy.wait_send()


def body(
    n, heads_axis,
    hidden_in, lengths, w_qkv, qk_gain, cache_keys, cache_values,
    w_out, norm_gain, w_gate_up, w_down,
):
    rows = lengths.shape[0]
    total_rows, feat = hidden_in.shape
    width = w_qkv.shape[2]
    heads = width // HEAD_DIM
    units = w_gate_up.shape[2]
    m = n // 2
    cu = units // CHUNKS
    half = HEAD_DIM // 2
    freqs = np.power(THETA, -(np.arange(half, dtype=np.float64) * 2.0 / HEAD_DIM))
    freqs = np.broadcast_to(np.concatenate([freqs, freqs]), (8, HEAD_DIM)).astype(np.float32)
    dma = pltpu.SemaphoreType.DMA
    vmem = pltpu.VMEM
    scratch = [
        vmem(w_qkv.shape, BF16), vmem(cache_keys.shape, BF16), vmem(cache_values.shape, BF16),
        vmem(w_out.shape, BF16), vmem(w_gate_up.shape, BF16), vmem(w_down.shape, BF16),
        vmem(w_out.shape[::-1], BF16), vmem(w_down.shape[::-1], BF16), dma((6,)),
        vmem(hidden_in.shape, BF16), vmem(qk_gain.shape, F32), vmem(norm_gain.shape, F32),
        vmem((8, HEAD_DIM), F32), dma((4,)),
        vmem((total_rows, feat), BF16),
        vmem((n, rows, width), BF16), vmem((n - 1, rows, width), BF16),
        vmem((n, rows, 2 * width), BF16), vmem((n - 1, rows, 2 * width), BF16),
        dma((2, n - 1)), dma((2, n - 1)),
        vmem((2, rows, HEAD_DIM), F32), vmem((2, heads_axis - 1, rows, HEAD_DIM), F32),
        dma((2, heads_axis - 1)), dma((2, heads_axis - 1)),
        vmem((heads * rows, cache_keys.shape[0]), F32),
        vmem((n, rows, width), BF16), dma((n - 1,)), dma((n - 1,)),
        vmem((2, heads_axis, total_rows, feat), BF16),
        dma((2, heads_axis - 1)), dma((2, heads_axis - 1)),
        vmem((2, 8, total_rows), F32), vmem((2, n - 1, 8, total_rows), F32),
        dma((2, n - 1)), dma((2, n - 1)),
        vmem((total_rows, feat), BF16),
        vmem((CHUNKS, 2, m, rows, 2 * cu), BF16), vmem((CHUNKS, m, rows, 2 * cu), BF16),
        vmem((CHUNKS, m, rows, 2 * cu), BF16), vmem((CHUNKS, m - 1, rows, 2 * cu), BF16),
        dma((CHUNKS,)), dma((CHUNKS,)), dma((CHUNKS, m - 1)), dma((CHUNKS, m - 1)),
        vmem((CHUNKS, n, rows, cu), BF16),
        dma((CHUNKS, m - 1)), dma((CHUNKS, m - 1)), dma((CHUNKS,)), dma((CHUNKS,)),
    ]
    in_vmem = pl.BlockSpec(memory_space=pltpu.VMEM)
    anywhere = pl.BlockSpec(memory_space=pl.ANY)
    outs = pl.pallas_call(
        functools.partial(kernel, n, heads_axis, feat * n),
        out_shape=(
            jax.ShapeDtypeStruct((total_rows, feat), BF16),
            jax.ShapeDtypeStruct((rows, width), BF16),
            jax.ShapeDtypeStruct((rows, width), BF16),
        ),
        in_specs=[pl.BlockSpec(memory_space=pltpu.SMEM)] + [anywhere] * 10,
        out_specs=(in_vmem,) * 3,
        scratch_shapes=scratch,
        compiler_params=pltpu.CompilerParams(
            collective_id=0, has_side_effects=True, vmem_limit_bytes=56 * 1024 * 1024
        ),
    )(
        lengths, hidden_in, qk_gain, norm_gain, jnp.asarray(freqs),
        w_qkv, cache_keys, cache_values, w_out, w_gate_up, w_down,
    )
    return pl.pallas_call(
        place_outputs,
        out_shape=tuple(jax.ShapeDtypeStruct(a.shape, a.dtype) for a in outs),
        in_specs=[in_vmem] * 3,
        out_specs=(in_vmem,) * 3,
    )(*outs)


def solution(mesh):
    return jax.shard_map(
        functools.partial(body, mesh.shape["req"], mesh.shape["head"]),
        mesh=mesh,
        in_specs=(
            P(None, "req"),
            P("req"),
            P(None, "req", "head"),
            P(None, "head"),
            P("req", "head"),
            P("req", "head"),
            P("req", "head"),
            P(None, "req"),
            P(None, "req", "head"),
            P("req", "head"),
        ),
        out_specs=(P(None, "req"), P("req", "head"), P("req", "head")),
        check_vma=False,
    )
```
